32 devices in a mesh: blk: 8 (over y, x, core), rep: 4 (over z).
Axes of the slice: x: 2, y: 2, z: 4, core: 2. Of those that a mesh axis runs over, the one named last changes fastest.
Arguments:
- node_feats: float32 [4096, 256], P('blk'), may hold values from -6 to 6
- operator_tiles: float32 [32, 16, 128, 128], P('blk', 'rep'), may hold values from -0.125 to 0.125
- tile_cols: int32 [32, 16], P('blk', 'rep'), may hold values from 0 to 31, as said below
- weight: float32 [256, 256], replicated, may hold values from -0.375 to 0.375
- layer_bias: float32 [256], replicated, may hold values from -3 to 3
- cotangent: float32 [4096, 256], P(('blk', 'rep')), may hold values from -6 to 6
Outputs:
- layer_out: float32 [4096, 256], P(('blk', 'rep'))
- grad_feats: float32 [4096, 256], P(('blk', 'rep'))
- grad_weight: float32 [256, 256], replicated
- grad_bias: float32 [256], replicated
The draws below stay inside these ranges and needn't reach their ends.
Inputs may be any that keep to these rules, and one draw needn't show every extreme that they name: `tile_cols`: owner of block j is j // 4, among 8 owners on a closed cycle. Slots r * 4 to (r + 1) * 4 - 1 of row block i name blocks whose owner lies at cycle distance (owner of i minus owner of the column, modulo the number of owners) from r * 2 to (r + 1) * 2 - 1. Slot 0 of row block i names block i itself. Entries may repeat within a row block.
All inputs are finite; a program needn't handle non-finite values.
Results may differ from the reference program's by a relative error of at most 0.0003.
Values sent between devices are 32-bit elements; how exact they have to be, the bound alone decides.
A program may use at most 64 MiB of HBM per device.

```python
import math
import jax
import jax.numpy as jnp
from jax import lax

BS = 128
D = 256
RBD = 4
SLOTS = 4
SEG = 2
KT = 16
NB = 32
N_NODES = 4096


def draw_tile_cols(key, part):
    owner_count = NB // RBD
    row_ids = jnp.arange(NB, dtype=jnp.int32)
    slot_indices = jnp.arange(KT, dtype=jnp.int32)
    key_dist, key_within = jax.random.split(key)
    offsets = jax.random.randint(key_dist, (NB, KT), 0, SEG, dtype=jnp.int32)
    distance = (slot_indices // SLOTS)[None, :] * SEG + offsets
    within = jax.random.randint(key_within, (NB, KT), 0, RBD, dtype=jnp.int32)
    column_owner = jnp.mod(row_ids[:, None] // RBD - distance, owner_count)
    columns = column_owner * RBD + within
    return columns.at[:, 0].set(row_ids)


def steps_of(key, shape, pieces, smallest, top_value):
    def one(position, shards_of):
        heights = jax.random.uniform(jax.random.fold_in(jax.random.fold_in(key, 6), position), (shards_of,), jnp.float32, smallest / len(pieces), top_value / len(pieces))
        return jnp.repeat(jnp.exp(heights), shape[position] // shards_of).reshape((-1,) + (1,) * (len(shape) - position - 1))

    factor_of = one(*pieces[0])
    for cut in pieces[1:]:
        factor_of = factor_of * one(*cut)
    return factor_of


def bell_draw(rng, dims, spread, limit, cuts=(), kind=jnp.bfloat16):
    result = spread * jax.random.normal(rng, dims, jnp.float32)
    if cuts:
        result = result * steps_of(rng, dims, cuts, -0.22, 0.18)
    return jnp.clip(result, -limit, limit).astype(kind)


def setup_inputs(seed: int = 0) -> dict:
    streams_of = jax.random.split(jax.random.key(seed), 7)
    node_feats = bell_draw(streams_of[0], (N_NODES, D), 1.0, 6.0, ((0, 8),), jnp.float32)
    operator_tiles = bell_draw(streams_of[1], (NB, KT, BS, BS), (BS * KT) ** -0.5, 0.125, ((0, 8), (1, 4)), jnp.float32)
    tile_cols = draw_tile_cols(jax.random.fold_in(streams_of[6], 71), 0)
    weight = bell_draw(streams_of[3], (D, D), D ** -0.5, 0.375, (), jnp.float32)
    layer_bias = bell_draw(streams_of[4], (D,), 0.5, 3.0, (), jnp.float32)
    cotangent = bell_draw(streams_of[5], (N_NODES, D), 1.0, 6.0, ((0, 32),), jnp.float32)
    return dict(node_feats=node_feats, operator_tiles=operator_tiles, tile_cols=tile_cols, weight=weight, layer_bias=layer_bias, cotangent=cotangent)


TOP_PRECISION = lax.Precision.HIGHEST

def reference(node_feats, operator_tiles, tile_cols, weight, layer_bias, cotangent):
    blocks_in = node_feats.reshape(NB, BS, D)

    def aggregate_row(pair):
        tile_set, column_ids = pair
        gathered = blocks_in[column_ids]
        return jnp.einsum('kab,kbd->ad', tile_set, gathered, precision=TOP_PRECISION)
    hidden = lax.map(aggregate_row, (operator_tiles, tile_cols)).reshape(N_NODES, D)
    pre_act = jnp.dot(hidden, weight, precision=TOP_PRECISION) + layer_bias
    negative = jnp.minimum(pre_act, 0.0)
    layer_out = jnp.where(pre_act > 0, pre_act, jnp.expm1(negative))
    grad_pre = cotangent * jnp.where(pre_act > 0, 1.0, jnp.exp(negative))
    grad_scale = 1.0 / math.sqrt(N_NODES)
    grad_weight = jnp.dot(hidden.T, grad_pre, precision=TOP_PRECISION) * grad_scale
    grad_bias = lax.optimization_barrier(jnp.sum(grad_pre, axis=0)) * grad_scale
    grad_hidden = jnp.dot(grad_pre, weight.T, precision=TOP_PRECISION).reshape(NB, BS, D)

    def scatter_row(accum, triple):
        tile_set, column_ids, rows_grad = triple
        terms = jnp.einsum('kab,ad->kbd', tile_set, rows_grad, precision=TOP_PRECISION)
        return (accum.at[column_ids].add(terms), None)
    grad_blocks, _ = lax.scan(scatter_row, jnp.zeros((NB, BS, D), node_feats.dtype), (operator_tiles, tile_cols, grad_hidden))
    return (layer_out, grad_blocks.reshape(N_NODES, D), grad_weight, grad_bias)
```

```python
import functools
import math

import jax
import jax.numpy as jnp
from jax import lax
from jax.experimental import pallas as pl
from jax.experimental.pallas import tpu as pltpu
from jax.sharding import PartitionSpec as P

TOP_PRECISION = lax.Precision.HIGHEST


def shifted_2(value, axis, steps):
    count = lax.axis_size(axis)
    pairs = [(source, (source + steps) % count) for source in range(count)]
    return lax.ppermute(value, axis, pairs)


def body(node_feats, operator_tiles, tile_cols, weight, layer_bias, cotangent):
    cycle_size = lax.axis_size("blk")
    rep_size = lax.axis_size("rep")
    window = cycle_size // rep_size
    position = lax.axis_index("blk")
    replica = lax.axis_index("rep")
    offset = replica * window
    blocks, slot_count, tile_size, _ = operator_tiles.shape
    width = node_feats.shape[1]
    row_count = blocks * tile_size
    owners = tile_cols // blocks
    within = tile_cols % blocks
    distance = jnp.mod(position - owners, cycle_size) - offset
    columns = jnp.arange(blocks, dtype=jnp.int32)
    sections = jnp.arange(window, dtype=jnp.int32)
    chosen = (
        (distance[:, :, None, None] == sections[None, None, :, None])
        & (within[:, :, None, None] == columns[None, None, None, :])
    ).astype(jnp.float32)

    def reshape_to_blocks(rows):
        return rows.reshape(blocks, tile_size, width)

    def store(stacked, section_no, current):
        return lax.dynamic_update_index_in_dim(stacked, reshape_to_blocks(current), section_no, 0)

    aligned = node_feats
    for bit_pos in range(rep_size.bit_length() - 1):
        shifted = shifted_2(aligned, "blk", window << bit_pos)
        aligned = jnp.where((replica >> bit_pos) % 2 == 1, shifted, aligned)
    empty = jnp.zeros((window, blocks, tile_size, width), jnp.float32)

    def advance(section_no, loop_state):
        current, stacked = loop_state
        current = shifted_2(current, "blk", 1)
        return (current, store(stacked, section_no, current))

    _, received = lax.fori_loop(1, window, advance, (aligned, store(empty, 0, aligned)))
    selected_tiles = jnp.einsum("iksc,scbd->ikbd", chosen, received, precision=TOP_PRECISION)
    partial_aggregate = jnp.einsum(
        "uzrj,uzje->ure", operator_tiles, selected_tiles, precision=TOP_PRECISION
    ).reshape(row_count, width)
    aggregated = lax.psum_scatter(partial_aggregate, "rep", scatter_dimension=0, tiled=True)
    pre_act = jnp.dot(aggregated, weight, precision=TOP_PRECISION) + layer_bias
    negative = jnp.minimum(pre_act, 0.0)
    layer_out = jnp.where(pre_act > 0, pre_act, jnp.expm1(negative))
    grad_pre = cotangent * jnp.where(pre_act > 0, 1.0, jnp.exp(negative))
    grad_scale = 1.0 / math.sqrt(row_count * cycle_size)
    grad_weight = (
        jnp.einsum("rd,re->de", aggregated, grad_pre, precision=TOP_PRECISION) * grad_scale
    )
    grad_bias = jnp.sum(grad_pre, axis=0) * grad_scale
    grad_weight, grad_bias = lax.psum((grad_weight, grad_bias), ("blk", "rep"))
    grad_hidden = jnp.einsum("re,de->rd", grad_pre, weight, precision=TOP_PRECISION)
    hidden_gradient = lax.all_gather(grad_hidden, "rep", axis=0, tiled=True)
    slot_terms = jnp.einsum(
        "xszt,xzc->xstc",
        operator_tiles,
        reshape_to_blocks(hidden_gradient),
        precision=TOP_PRECISION,
    )
    sorted_terms = jnp.einsum("iksc,ikbd->scbd", chosen, slot_terms, precision=TOP_PRECISION)

    def adjoint_term(section_no):
        return lax.dynamic_index_in_dim(sorted_terms, section_no, 0, keepdims=False).reshape(
            row_count, width
        )

    def retreat(counter, running):
        moved = shifted_2(running, "blk", -1)
        return moved + adjoint_term(window - 1 - counter)

    adjoint = lax.fori_loop(1, window, retreat, adjoint_term(window - 1))
    for bit_pos in range(rep_size.bit_length() - 1):
        returned = shifted_2(adjoint, "blk", -(window << bit_pos))
        adjoint = jnp.where((replica >> bit_pos) % 2 == 1, returned, adjoint)
    grad_feats = lax.psum_scatter(adjoint, "rep", scatter_dimension=0, tiled=True)
    return (layer_out, grad_feats, grad_weight, grad_bias)


F32, BF16 = jnp.float32, jnp.bfloat16
HALVES = 2


def split(value):
    high = value.astype(BF16)
    return high, (value - high.astype(F32)).astype(BF16)


def dot3(a, b):
    def product(x, y):
        return jnp.dot(x, y, preferred_element_type=F32)

    return product(a[0], b[0]) + (product(a[0], b[1]) + product(a[1], b[0]))


def kernel(
    n, m, feats, tiles, cols, weight, bias, cot,
    out, gfeats, gweight, gbias,
    xs, s_hi, s_lo, st_hi, st_lo, hpart, hrecv, grad, adj, fold, total, frecv,
    gws, gwr, gwz, gfin, send_sem, recv_sem,
):
    p, r = lax.axis_index("blk"), lax.axis_index("rep")
    blocks, slots, size, _ = tiles.shape
    rows = blocks * size
    part, width = cot.shape
    cw = width // HALVES
    piece = width // n
    even = lax.rem(p, 2) == 0
    odd = jnp.logical_not(even)
    moved = r > 0
    always = None

    barrier = pltpu.get_barrier_semaphore()
    for d in range(1, n):
        pl.semaphore_signal(barrier, inc=1, device_id={"blk": lax.rem(p + d, n), "rep": r})
    for d in range(1, m):
        pl.semaphore_signal(barrier, inc=1, device_id={"blk": p, "rep": lax.rem(r + d, m)})
    pl.semaphore_wait(barrier, n - 1 + m - 1)

    keys, started = {}, []

    def when(cond, action):
        if cond is None:
            action()
        else:
            pl.when(cond)(action)

    def copy(name, src, dst, blk, rep):
        key = keys.setdefault(name, len(keys))
        return pltpu.make_async_remote_copy(
            src_ref=src,
            dst_ref=dst,
            send_sem=send_sem.at[key],
            recv_sem=recv_sem.at[key],
            device_id={"blk": blk, "rep": rep},
        )

    def start(made, cond=always):
        started.append((made, cond))
        when(cond, made.start)

    def half(c):
        return pl.ds(c * cw, cw)

    ahead = lax.rem(p + 2 * r, n)
    after = lax.rem(p + 2 * r + 1, n)
    nxt = lax.rem(p + 1, n)
    first = [copy(("a", c), feats.at[:, half(c)], xs.at[0, c], ahead, r) for c in range(HALVES)]
    second_odd = [copy(("b", c), feats.at[:, half(c)], xs.at[1, c], after, r) for c in range(HALVES)]
    second_even = [copy(("b", c), xs.at[0, c], xs.at[1, c], nxt, r) for c in range(HALVES)]

    for c in range(HALVES):
        start(first[c], moved)
        start(second_odd[c], odd)

    @pl.when(r == 0)
    def _():
        for c in range(HALVES):
            xs[0, c] = feats[:, half(c)]

    for s in range(2):
        owner = lax.rem(p - 2 * r - s + 2 * n, n)
        for b in range(blocks):
            name = owner * blocks + b
            at = slice((s * blocks + b) * size, (s * blocks + b + 1) * size)
            for i in range(blocks):
                tile = jnp.zeros((size, size), F32)
                for k in range(slots):
                    tile = tile + tiles[i, k] * jnp.where(cols[i, k] == name, 1.0, 0.0)
                high, low = split(tile)
                s_hi[i * size : (i + 1) * size, at] = high
                s_lo[i * size : (i + 1) * size, at] = low
                high, low = split(tile.T)
                st_hi[at, i * size : (i + 1) * size] = high
                st_lo[at, i * size : (i + 1) * size] = low

    w = split(weight[...])
    wt = split(weight[...].T)

    hsends = []
    for c in range(HALVES):
        when(moved, first[c].wait_recv)
        start(second_even[c], even)
        acc = dot3((s_hi[:, :rows], s_lo[:, :rows]), split(xs[0, c]))
        second_odd[c].wait_recv()
        acc = acc + dot3((s_hi[:, rows:], s_lo[:, rows:]), split(xs[1, c]))
        hpart[c] = acc.reshape(m, part, cw)
        for d in range(m - 1, 0, -1):
            to = lax.rem(r + d, m)
            made = copy(("c", c, d), hpart.at[c, to], hrecv.at[c, d - 1], p, to)
            start(made)
            hsends.append(made)
    for made in hsends:
        made.wait_recv()
    agg = jnp.concatenate(
        [hpart[c, r] + ((hrecv[c, 0] + hrecv[c, 1]) + hrecv[c, 2]) for c in range(HALVES)], axis=1
    )

    pre = dot3(split(agg), w) + bias[...]
    exped = jnp.exp(jnp.minimum(pre, 0.0))
    gpre = cot[...] * jnp.where(pre > 0, 1.0, exped)
    gpre_parts = split(gpre)
    gsends = []
    for c in range(HALVES):
        columns = slice(c * cw, (c + 1) * cw)
        grad[c, r] = dot3(gpre_parts, (wt[0][:, columns], wt[1][:, columns]))
        made_c = []
        for d in range(m - 1, 0, -1):
            to = lax.rem(r + d, m)
            made = copy(("d", c, d), grad.at[c, r], grad.at[c, r], p, to)
            start(made)
            made_c.append(made)
        gsends.append(made_c)
    out[...] = jnp.where(pre > 0, pre, exped - 1.0)

    gw = dot3(split(agg.T), gpre_parts)
    gb = jnp.broadcast_to(jnp.sum(gpre, axis=0, keepdims=True), (8, width))
    for q in range(n):
        gws[q, :piece] = gw[q * piece : (q + 1) * piece]
        gws[q, piece:] = gb
    gwr[p] = gws[p]
    esends = []
    for d in range(1, n):
        to = lax.rem(p + d, n)
        made = copy(("e", d), gws.at[to], gwr.at[p], to, r)
        start(made)
        esends.append(made)

    def weight_sums():
        for made in esends:
            made.wait_recv()
        total_p = gwr[0]
        for q in range(1, n):
            total_p = total_p + gwr[q]
        gwz[r] = total_p
        made_z = []
        for d in range(m - 1, 0, -1):
            to = lax.rem(r + d, m)
            made = copy(("m", d), gwz.at[r], gwz.at[r], p, to)
            start(made)
            made_z.append(made)
        return made_z

    scale = 1.0 / math.sqrt(rows * n)

    def weight_gather(made_z):
        for made in made_z:
            made.wait_recv()
        whole = gwz[0]
        for q in range(1, m):
            whole = whole + gwz[q]
        gfin[p] = whole[:piece] * scale
        gbias[...] = whole[piece : piece + 1] * scale
        made_n = []
        for d in range(1, n):
            to = lax.rem(p + d, n)
            made = copy(("n", d), gfin.at[p], gfin.at[p], to, r)
            start(made)
            made_n.append(made)
        return made_n

    back = lax.rem(p - 2 * r + n, n)
    before = lax.rem(p - 2 * r - 1 + 2 * n, n)
    prv = lax.rem(p - 1 + n, n)
    fold_even = [copy(("f", c), adj.at[1, c], fold.at[c], before, r) for c in range(HALVES)]
    fold_odd = [copy(("f", c), adj.at[1, c], fold.at[c], prv, r) for c in range(HALVES)]
    last = [copy(("k", c), adj.at[0, c], total.at[c], back, r) for c in range(HALVES)]

    def adjoint(c):
        for made in gsends[c]:
            made.wait_recv()
        g = split(grad[c].reshape(rows, cw))
        adj[1, c] = dot3((st_hi[rows:], st_lo[rows:]), g).reshape(m, part, cw)
        start(fold_odd[c], odd)
        start(fold_even[c], even)
        adj[0, c] = dot3((st_hi[:rows], st_lo[:rows]), g).reshape(m, part, cw)

        @pl.when(even)
        def _():
            fold_even[c].wait_recv()
            adj[0, c] = adj[0, c] + fold[c]

        start(last[c], moved)

    def adjoint_reduce(c):
        when(moved, last[c].wait_recv)

        @pl.when(r == 0)
        def _():
            total[c] = adj[0, c]

        @pl.when(odd)
        def _():
            fold_even[c].wait_recv()
            total[c] = total[c] + fold[c]

        made_c = []
        for d in range(m - 1, 0, -1):
            to = lax.rem(r + d, m)
            made = copy(("l", c, d), total.at[c, to], frecv.at[c, d - 1], p, to)
            start(made)
            made_c.append(made)
        return made_c

    adjoint(0)
    made_z = weight_sums()
    adjoint(1)
    lsends = [adjoint_reduce(0)]
    made_n = weight_gather(made_z)
    lsends.append(adjoint_reduce(1))
    for c in range(HALVES):
        if c == 1:
            for made in made_n:
                made.wait_recv()
            gweight[...] = gfin[...].reshape(width, width)
        for made in lsends[c]:
            made.wait_recv()
        gfeats[:, half(c)] = total[c, r] + ((frecv[c, 0] + frecv[c, 1]) + frecv[c, 2])
    for made, cond in started:
        when(cond, made.wait_send)


def fast_body(n, m, node_feats, operator_tiles, tile_cols, weight, layer_bias, cotangent):
    blocks, _, size, _ = operator_tiles.shape
    rows = blocks * size
    part, width = cotangent.shape
    cw = width // HALVES
    piece = width // n
    copies = HALVES * (2 + 3 * (m - 1) + 2) + 2 * (n - 1) + (m - 1)
    vmem = pl.BlockSpec(memory_space=pltpu.VMEM)
    smem = pl.BlockSpec(memory_space=pltpu.SMEM)
    shape = jax.ShapeDtypeStruct
    quarter = (HALVES, m, part, cw)
    result = pl.pallas_call(
        functools.partial(kernel, n, m),
        out_shape=(
            shape((part, width), F32),
            shape((part, width), F32),
            shape((width, width), F32),
            shape((1, width), F32),
        ),
        in_specs=[vmem, vmem, smem, vmem, vmem, vmem],
        out_specs=(vmem,) * 4,
        scratch_shapes=[
            pltpu.VMEM((2, HALVES, rows, cw), F32),
            pltpu.VMEM((rows, 2 * rows), BF16),
            pltpu.VMEM((rows, 2 * rows), BF16),
            pltpu.VMEM((2 * rows, rows), BF16),
            pltpu.VMEM((2 * rows, rows), BF16),
            pltpu.VMEM(quarter, F32),
            pltpu.VMEM((HALVES, m - 1, part, cw), F32),
            pltpu.VMEM(quarter, F32),
            pltpu.VMEM((2,) + quarter, F32),
            pltpu.VMEM(quarter, F32),
            pltpu.VMEM(quarter, F32),
            pltpu.VMEM((HALVES, m - 1, part, cw), F32),
            pltpu.VMEM((n, piece + 8, width), F32),
            pltpu.VMEM((n, piece + 8, width), F32),
            pltpu.VMEM((m, piece + 8, width), F32),
            pltpu.VMEM((n, piece, width), F32),
            pltpu.SemaphoreType.DMA((copies,)),
            pltpu.SemaphoreType.DMA((copies,)),
        ],
        compiler_params=pltpu.CompilerParams(
            collective_id=0, has_side_effects=True, vmem_limit_bytes=48 * 1024 * 1024
        ),
    )(node_feats, operator_tiles, tile_cols, weight, layer_bias.reshape(1, width), cotangent)
    layer_out, grad_feats, grad_weight, grad_bias = result
    return layer_out, grad_feats, grad_weight, grad_bias.reshape(width)


def solution(mesh):
    n, m = mesh.shape["blk"], mesh.shape["rep"]
    fits = n == 2 * m and m == 4
    return jax.shard_map(
        functools.partial(fast_body, n, m) if fits else body,
        mesh=mesh,
        in_specs=(
            P("blk", None),
            P("blk", "rep", None, None),
            P("blk", "rep"),
            P(),
            P(),
            P(("blk", "rep"), None),
        ),
        out_specs=(P(("blk", "rep"), None), P(("blk", "rep"), None), P(), P()),
        check_vma=False,
    )
```

```python
import functools
import math

import jax
import jax.numpy as jnp
from jax import lax
from jax.experimental import pallas as pl
from jax.experimental.pallas import tpu as pltpu
from jax.sharding import PartitionSpec as P

TOP_PRECISION = lax.Precision.HIGHEST


def shifted_2(value, axis, steps):
    count = lax.axis_size(axis)
    pairs = [(source, (source + steps) % count) for source in range(count)]
    return lax.ppermute(value, axis, pairs)


def body(node_feats, operator_tiles, tile_cols, weight, layer_bias, cotangent):
    cycle_size = lax.axis_size("blk")
    rep_size = lax.axis_size("rep")
    window = cycle_size // rep_size
    position = lax.axis_index("blk")
    replica = lax.axis_index("rep")
    offset = replica * window
    blocks, slot_count, tile_size, _ = operator_tiles.shape
    width = node_feats.shape[1]
    row_count = blocks * tile_size
    owners = tile_cols // blocks
    within = tile_cols % blocks
    distance = jnp.mod(position - owners, cycle_size) - offset
    columns = jnp.arange(blocks, dtype=jnp.int32)
    sections = jnp.arange(window, dtype=jnp.int32)
    chosen = (
        (distance[:, :, None, None] == sections[None, None, :, None])
        & (within[:, :, None, None] == columns[None, None, None, :])
    ).astype(jnp.float32)

    def reshape_to_blocks(rows):
        return rows.reshape(blocks, tile_size, width)

    def store(stacked, section_no, current):
        return lax.dynamic_update_index_in_dim(stacked, reshape_to_blocks(current), section_no, 0)

    aligned = node_feats
    for bit_pos in range(rep_size.bit_length() - 1):
        shifted = shifted_2(aligned, "blk", window << bit_pos)
        aligned = jnp.where((replica >> bit_pos) % 2 == 1, shifted, aligned)
    empty = jnp.zeros((window, blocks, tile_size, width), jnp.float32)

    def advance(section_no, loop_state):
        current, stacked = loop_state
        current = shifted_2(current, "blk", 1)
        return (current, store(stacked, section_no, current))

    _, received = lax.fori_loop(1, window, advance, (aligned, store(empty, 0, aligned)))
    selected_tiles = jnp.einsum("iksc,scbd->ikbd", chosen, received, precision=TOP_PRECISION)
    partial_aggregate = jnp.einsum(
        "uzrj,uzje->ure", operator_tiles, selected_tiles, precision=TOP_PRECISION
    ).reshape(row_count, width)
    aggregated = lax.psum_scatter(partial_aggregate, "rep", scatter_dimension=0, tiled=True)
    pre_act = jnp.dot(aggregated, weight, precision=TOP_PRECISION) + layer_bias
    negative = jnp.minimum(pre_act, 0.0)
    layer_out = jnp.where(pre_act > 0, pre_act, jnp.expm1(negative))
    grad_pre = cotangent * jnp.where(pre_act > 0, 1.0, jnp.exp(negative))
    grad_scale = 1.0 / math.sqrt(row_count * cycle_size)
    grad_weight = (
        jnp.einsum("rd,re->de", aggregated, grad_pre, precision=TOP_PRECISION) * grad_scale
    )
    grad_bias = jnp.sum(grad_pre, axis=0) * grad_scale
    grad_weight, grad_bias = lax.psum((grad_weight, grad_bias), ("blk", "rep"))
    grad_hidden = jnp.einsum("re,de->rd", grad_pre, weight, precision=TOP_PRECISION)
    hidden_gradient = lax.all_gather(grad_hidden, "rep", axis=0, tiled=True)
    slot_terms = jnp.einsum(
        "xszt,xzc->xstc",
        operator_tiles,
        reshape_to_blocks(hidden_gradient),
        precision=TOP_PRECISION,
    )
    sorted_terms = jnp.einsum("iksc,ikbd->scbd", chosen, slot_terms, precision=TOP_PRECISION)

    def adjoint_term(section_no):
        return lax.dynamic_index_in_dim(sorted_terms, section_no, 0, keepdims=False).reshape(
            row_count, width
        )

    def retreat(counter, running):
        moved = shifted_2(running, "blk", -1)
        return moved + adjoint_term(window - 1 - counter)

    adjoint = lax.fori_loop(1, window, retreat, adjoint_term(window - 1))
    for bit_pos in range(rep_size.bit_length() - 1):
        returned = shifted_2(adjoint, "blk", -(window << bit_pos))
        adjoint = jnp.where((replica >> bit_pos) % 2 == 1, returned, adjoint)
    grad_feats = lax.psum_scatter(adjoint, "rep", scatter_dimension=0, tiled=True)
    return (layer_out, grad_feats, grad_weight, grad_bias)


F32, BF16 = jnp.float32, jnp.bfloat16
HALVES = 2


def split(value):
    high = value.astype(BF16)
    return high, (value - high.astype(F32)).astype(BF16)


def dot3(a, b):
    def product(x, y):
        return jnp.dot(x, y, preferred_element_type=F32)

    return product(a[0], b[0]) + (product(a[0], b[1]) + product(a[1], b[0]))


def kernel(
    n, m, feats, tiles_hbm, cols_hbm, weight_hbm, bias_hbm, cot_hbm,
    out, gfeats, gweight, gbias,
    tiles, cols, weight, bias, cot,
    xs, s_hi, s_lo, st_hi, st_lo, hpart, hrecv, grad, adj, fold, extra, total, frecv,
    gws, gwr, gwz, gfin, send_sem, recv_sem, load_sem,
):
    p, r = lax.axis_index("blk"), lax.axis_index("rep")
    blocks, slots, size, _ = tiles.shape
    rows = blocks * size
    part, width = cot.shape
    cw = width // HALVES
    piece = width // n
    kind = lax.rem(p, 4)
    even = lax.rem(p, 2) == 0
    odd = jnp.logical_not(even)
    moved = r > 0
    always = None

    def both(x, y):
        return jnp.logical_and(x, y)

    def but(x, y):
        return jnp.logical_and(x, jnp.logical_not(y))

    def when(cond, action):
        if cond is None:
            action()
        else:
            pl.when(cond)(action)

    near_from = both(r == 1, kind == 2)
    near_to = both(r == 1, kind == 1)
    above = both(r == 3, kind == 3)
    below = both(r == 2, kind == 2)
    nxt = lax.rem(p + 1, n)
    prv = lax.rem(p - 1 + n, n)

    pairs = [
        (tiles_hbm, tiles),
        (cols_hbm, cols),
        (weight_hbm, weight),
        (bias_hbm, bias),
        (cot_hbm, cot),
    ]
    loads = [
        pltpu.make_async_copy(src, dst, load_sem.at[i]) for i, (src, dst) in enumerate(pairs)
    ]
    for made in loads:
        made.start()

    barrier = pltpu.get_barrier_semaphore()
    for d in range(1, n):
        pl.semaphore_signal(barrier, inc=1, device_id={"blk": lax.rem(p + d, n), "rep": r})
    for d in range(1, m):
        pl.semaphore_signal(barrier, inc=1, device_id={"blk": p, "rep": lax.rem(r + d, m)})

    @pl.when(above)
    def _():
        pl.semaphore_signal(barrier, inc=1, device_id={"blk": prv, "rep": 2})

    @pl.when(below)
    def _():
        pl.semaphore_signal(barrier, inc=1, device_id={"blk": nxt, "rep": 3})

    pl.semaphore_wait(barrier, n + m - 2 + jnp.where(jnp.logical_or(above, below), 1, 0))

    keys, started = {}, []

    def copy(name, src, dst, blk, rep):
        key = keys.setdefault(name, len(keys))
        return pltpu.make_async_remote_copy(
            src_ref=src,
            dst_ref=dst,
            send_sem=send_sem.at[key],
            recv_sem=recv_sem.at[key],
            device_id={"blk": blk, "rep": rep},
        )

    def start(made, cond=always):
        started.append((made, cond))
        when(cond, made.start)

    def half(c):
        return pl.ds(c * cw, cw)

    ahead = lax.rem(p + 2 * r, n)
    after = lax.rem(p + 2 * r + 1, n)
    to_ahead = but(moved, both(r == 1, lax.rem(ahead, 4) == 1))
    to_after = but(odd, both(r == 2, lax.rem(after, 4) == 2))

    def to_first(c, src, blk, rep):
        return copy(("a", c), src, xs.at[0, c], blk, rep)

    def to_second(c, src, blk, rep):
        return copy(("b", c), src, xs.at[1, c], blk, rep)

    for c in range(HALVES):
        start(to_first(c, feats.at[:, half(c)], ahead, r), to_ahead)
        start(to_second(c, feats.at[:, half(c)], after, r), to_after)
    own = [
        pltpu.make_async_copy(feats.at[:, half(c)], xs.at[0, c], load_sem.at[len(pairs) + c])
        for c in range(HALVES)
    ]

    @pl.when(r == 0)
    def _():
        for c in range(HALVES):
            own[c].start()

    for made in loads:
        made.wait()
    for s in range(2):
        owner = lax.rem(p - 2 * r - s + 2 * n, n)
        for b in range(blocks):
            name = owner * blocks + b
            at = slice((s * blocks + b) * size, (s * blocks + b + 1) * size)
            for i in range(blocks):
                tile = jnp.zeros((size, size), F32)
                for k in range(slots):
                    tile = tile + tiles[i, k] * jnp.where(cols[i, k] == name, 1.0, 0.0)
                high, low = split(tile)
                s_hi[i * size : (i + 1) * size, at] = high
                s_lo[i * size : (i + 1) * size, at] = low
                high, low = split(tile.T)
                st_hi[at, i * size : (i + 1) * size] = high
                st_lo[at, i * size : (i + 1) * size] = low

    def take_first(c):
        @pl.when(moved)
        def _():
            to_first(c, xs.at[0, c], p, r).wait_recv()

        @pl.when(r == 0)
        def _():
            own[c].wait()

        start(to_second(c, xs.at[0, c], nxt, r), even)
        start(to_second(c, xs.at[0, c], prv, r - 1), above)

    def product(c, s):
        at = slice(s * rows, (s + 1) * rows)
        return dot3((s_hi[:, at], s_lo[:, at]), split(xs[s, c]))

    hsends = []

    def aggregate_sends(c):
        for d in range(m - 1, 0, -1):
            to = lax.rem(r + d, m)
            made = copy(("c", c, d), hpart.at[c, to], hrecv.at[c, d - 1], p, to)
            start(made)
            hsends.append(made)

    for c in range(HALVES):
        @pl.when(near_from)
        def _():
            to_second(c, xs.at[1, c], p, r).wait_recv()
            to_first(c, xs.at[1, c], prv, r).start()

        take_first(c)
        acc = product(c, 0)
        pl.when(jnp.logical_not(near_from))(to_second(c, xs.at[1, c], p, r).wait_recv)
        acc = acc + product(c, 1)
        hpart[c] = acc.reshape(m, part, cw)
        aggregate_sends(c)
    for c in range(HALVES):
        started.append((to_first(c, xs.at[1, c], prv, r), near_from))
    for made in hsends:
        made.wait_recv()
    agg = jnp.concatenate(
        [hpart[c, r] + ((hrecv[c, 0] + hrecv[c, 1]) + hrecv[c, 2]) for c in range(HALVES)], axis=1
    )

    w = split(weight[...])
    wt = split(weight[...].T)
    pre = dot3(split(agg), w) + bias[...]
    exped = jnp.exp(jnp.minimum(pre, 0.0))
    gpre = cot[...] * jnp.where(pre > 0, 1.0, exped)
    gpre_parts = split(gpre)
    gsends = []
    for c in range(HALVES):
        columns = slice(c * cw, (c + 1) * cw)
        grad[c, r] = dot3(gpre_parts, (wt[0][:, columns], wt[1][:, columns]))
        made_c = []
        for d in range(m - 1, 0, -1):
            to = lax.rem(r + d, m)
            made = copy(("d", c, d), grad.at[c, r], grad.at[c, r], p, to)
            start(made)
            made_c.append(made)
        gsends.append(made_c)
    out[...] = jnp.where(pre > 0, pre, exped - 1.0)

    gw = dot3(split(agg.T), gpre_parts)
    gb = jnp.broadcast_to(jnp.sum(gpre, axis=0, keepdims=True), (8, width))
    for q in range(n):
        gws[q, :piece] = gw[q * piece : (q + 1) * piece]
        gws[q, piece:] = gb
    gwr[p] = gws[p]
    esends = []
    for d in range(1, n):
        to = lax.rem(p + d, n)
        made = copy(("e", d), gws.at[to], gwr.at[p], to, r)
        start(made)
        esends.append(made)

    def weight_sums():
        for made in esends:
            made.wait_recv()
        total_p = gwr[0]
        for q in range(1, n):
            total_p = total_p + gwr[q]
        gwz[r] = total_p
        made_z = []
        for d in range(m - 1, 0, -1):
            to = lax.rem(r + d, m)
            made = copy(("m", d), gwz.at[r], gwz.at[r], p, to)
            start(made)
            made_z.append(made)
        return made_z

    scale = 1.0 / math.sqrt(rows * n)

    def weight_gather(made_z):
        for made in made_z:
            made.wait_recv()
        whole = gwz[0]
        for q in range(1, m):
            whole = whole + gwz[q]
        gfin[p] = whole[:piece] * scale
        gbias[...] = whole[piece : piece + 1] * scale
        made_n = []
        for d in range(1, n):
            to = lax.rem(p + d, n)
            made = copy(("n", d), gfin.at[p], gfin.at[p], to, r)
            start(made)
            made_n.append(made)
        return made_n

    back = lax.rem(p - 2 * r + n, n)
    before = lax.rem(p - 2 * r - 1 + 2 * n, n)
    order = [m - 1 - j for j in range(m)]

    def place(d):
        return lax.rem(r + d, m)

    def to_fold(c, d, blk):
        b = place(d)
        return copy(("f", c, d), adj.at[1, c, b], fold.at[c, b], blk, r)

    def to_near(c, d):
        b = place(d)
        return copy(("g", c, d), adj.at[0, c, b], extra.at[c, b], nxt, r)

    def to_above(c, b):
        return copy(("h", c, b), adj.at[1, c, b], extra.at[c, b], nxt, r + 1)

    def to_total(c, d):
        b = place(d)
        return copy(("k", c, d), adj.at[0, c, b], total.at[c, b], back, r)

    plain_second = but(but(even, below), near_from)
    plain_first = but(but(both(odd, moved), near_to), above)

    def adjoint(c):
        for made in gsends[c]:
            made.wait_recv()
        g = split(grad[c].reshape(rows, cw))
        adj[1, c] = dot3((st_hi[rows:], st_lo[rows:]), g).reshape(m, part, cw)
        for d in order:
            start(to_fold(c, d, prv), odd)
            start(to_fold(c, d, before), plain_second)
        for b in range(m):
            start(to_above(c, b), below)
        adj[0, c] = dot3((st_hi[:rows], st_lo[:rows]), g).reshape(m, part, cw)
        for d in order:
            start(to_near(c, d), near_to)
            start(to_total(c, d), plain_first)

        @pl.when(even)
        def _():
            for d in order:
                b = place(d)
                to_fold(c, d, prv).wait_recv()
                adj[0, c, b] = adj[0, c, b] + fold[c, b]
                pl.when(moved)(to_total(c, d).start)

        @pl.when(above)
        def _():
            for d in order:
                b = (3 + d) % m
                to_above(c, b).wait_recv()
                adj[0, c, b] = adj[0, c, b] + extra[c, b]
                to_total(c, d).start()

        @pl.when(near_from)
        def _():
            for d in order:
                b = place(d)
                to_near(c, d).wait_recv()
                adj[1, c, b] = adj[1, c, b] + extra[c, b]
                to_fold(c, d, before).start()

        for d in order:
            started.append((to_total(c, d), both(even, moved)))
            started.append((to_total(c, d), above))
            started.append((to_fold(c, d, before), near_from))

    from_total = but(moved, both(r == 1, kind == 3))
    from_fold = but(odd, both(r == 2, kind == 1))

    def adjoint_reduce(c):
        made_c = []
        for d in order:
            b = place(d)

            @pl.when(from_total)
            def _():
                to_total(c, d).wait_recv()

            @pl.when(r == 0)
            def _():
                total[c, b] = adj[0, c, b]

            @pl.when(from_fold)
            def _():
                to_fold(c, d, prv).wait_recv()

                @pl.when(from_total)
                def _():
                    total[c, b] = total[c, b] + fold[c, b]

                @pl.when(r == 0)
                def _():
                    total[c, b] = total[c, b] + fold[c, b]

                @pl.when(both(r == 1, kind == 3))
                def _():
                    total[c, b] = fold[c, b]

            if d:
                made = copy(("l", c, d), total.at[c, b], frecv.at[c, d - 1], p, b)
                start(made)
                made_c.append(made)
        return made_c

    adjoint(0)
    made_z = weight_sums()
    adjoint(1)
    lsends = [adjoint_reduce(0)]
    made_n = weight_gather(made_z)
    lsends.append(adjoint_reduce(1))
    for c in range(HALVES):
        if c == 1:
            for made in made_n:
                made.wait_recv()
            gweight[...] = gfin[...].reshape(width, width)
        for made in lsends[c]:
            made.wait_recv()
        gfeats[:, half(c)] = total[c, r] + ((frecv[c, 0] + frecv[c, 1]) + frecv[c, 2])
    for made, cond in started:
        when(cond, made.wait_send)


def fast_body(n, m, node_feats, operator_tiles, tile_cols, weight, layer_bias, cotangent):
    blocks, _, size, _ = operator_tiles.shape
    rows = blocks * size
    part, width = cotangent.shape
    cw = width // HALVES
    piece = width // n
    copies = HALVES * (2 + 3 * (m - 1) + 4 * m) + 2 * (n - 1) + (m - 1)
    vmem = pl.BlockSpec(memory_space=pltpu.VMEM)
    shape = jax.ShapeDtypeStruct
    quarter = (HALVES, m, part, cw)
    result = pl.pallas_call(
        functools.partial(kernel, n, m),
        out_shape=(
            shape((part, width), F32),
            shape((part, width), F32),
            shape((width, width), F32),
            shape((1, width), F32),
        ),
        in_specs=[pl.BlockSpec(memory_space=pltpu.HBM)] * 6,
        out_specs=(vmem,) * 4,
        scratch_shapes=[
            pltpu.VMEM(operator_tiles.shape, F32),
            pltpu.SMEM(tile_cols.shape, jnp.int32),
            pltpu.VMEM((width, width), F32),
            pltpu.VMEM((1, width), F32),
            pltpu.VMEM((part, width), F32),
            pltpu.VMEM((2, HALVES, rows, cw), F32),
            pltpu.VMEM((rows, 2 * rows), BF16),
            pltpu.VMEM((rows, 2 * rows), BF16),
            pltpu.VMEM((2 * rows, rows), BF16),
            pltpu.VMEM((2 * rows, rows), BF16),
            pltpu.VMEM(quarter, F32),
            pltpu.VMEM((HALVES, m - 1, part, cw), F32),
            pltpu.VMEM(quarter, F32),
            pltpu.VMEM((2,) + quarter, F32),
            pltpu.VMEM(quarter, F32),
            pltpu.VMEM(quarter, F32),
            pltpu.VMEM(quarter, F32),
            pltpu.VMEM((HALVES, m - 1, part, cw), F32),
            pltpu.VMEM((n, piece + 8, width), F32),
            pltpu.VMEM((n, piece + 8, width), F32),
            pltpu.VMEM((m, piece + 8, width), F32),
            pltpu.VMEM((n, piece, width), F32),
            pltpu.SemaphoreType.DMA((copies,)),
            pltpu.SemaphoreType.DMA((copies,)),
            pltpu.SemaphoreType.DMA((5 + HALVES,)),
        ],
        compiler_params=pltpu.CompilerParams(
            collective_id=0, has_side_effects=True, vmem_limit_bytes=63 * 1024 * 1024
        ),
    )(node_feats, operator_tiles, tile_cols, weight, layer_bias.reshape(1, width), cotangent)
    layer_out, grad_feats, grad_weight, grad_bias = result
    return layer_out, grad_feats, grad_weight, grad_bias.reshape(width)


def solution(mesh):
    n, m = mesh.shape["blk"], mesh.shape["rep"]
    fits = n == 2 * m and m == 4
    return jax.shard_map(
        functools.partial(fast_body, n, m) if fits else body,
        mesh=mesh,
        in_specs=(
            P("blk", None),
            P("blk", "rep", None, None),
            P("blk", "rep"),
            P(),
            P(),
            P(("blk", "rep"), None),
        ),
        out_specs=(P(("blk", "rep"), None), P(("blk", "rep"), None), P(), P()),
        check_vma=False,
    )
```

```python
import functools
import math

import jax
import jax.numpy as jnp
from jax import lax
from jax.experimental import pallas as pl
from jax.experimental.pallas import tpu as pltpu
from jax.sharding import PartitionSpec as P

TOP_PRECISION = lax.Precision.HIGHEST


def shifted_2(value, axis, steps):
    count = lax.axis_size(axis)
    pairs = [(source, (source + steps) % count) for source in range(count)]
    return lax.ppermute(value, axis, pairs)


def body(node_feats, operator_tiles, tile_cols, weight, layer_bias, cotangent):
    cycle_size = lax.axis_size("blk")
    rep_size = lax.axis_size("rep")
    window = cycle_size // rep_size
    position = lax.axis_index("blk")
    replica = lax.axis_index("rep")
    offset = replica * window
    blocks, slot_count, tile_size, _ = operator_tiles.shape
    width = node_feats.shape[1]
    row_count = blocks * tile_size
    owners = tile_cols // blocks
    within = tile_cols % blocks
    distance = jnp.mod(position - owners, cycle_size) - offset
    columns = jnp.arange(blocks, dtype=jnp.int32)
    sections = jnp.arange(window, dtype=jnp.int32)
    chosen = (
        (distance[:, :, None, None] == sections[None, None, :, None])
        & (within[:, :, None, None] == columns[None, None, None, :])
    ).astype(jnp.float32)

    def reshape_to_blocks(rows):
        return rows.reshape(blocks, tile_size, width)

    def store(stacked, section_no, current):
        return lax.dynamic_update_index_in_dim(stacked, reshape_to_blocks(current), section_no, 0)

    aligned = node_feats
    for bit_pos in range(rep_size.bit_length() - 1):
        shifted = shifted_2(aligned, "blk", window << bit_pos)
        aligned = jnp.where((replica >> bit_pos) % 2 == 1, shifted, aligned)
    empty = jnp.zeros((window, blocks, tile_size, width), jnp.float32)

    def advance(section_no, loop_state):
        current, stacked = loop_state
        current = shifted_2(current, "blk", 1)
        return (current, store(stacked, section_no, current))

    _, received = lax.fori_loop(1, window, advance, (aligned, store(empty, 0, aligned)))
    selected_tiles = jnp.einsum("iksc,scbd->ikbd", chosen, received, precision=TOP_PRECISION)
    partial_aggregate = jnp.einsum(
        "uzrj,uzje->ure", operator_tiles, selected_tiles, precision=TOP_PRECISION
    ).reshape(row_count, width)
    aggregated = lax.psum_scatter(partial_aggregate, "rep", scatter_dimension=0, tiled=True)
    pre_act = jnp.dot(aggregated, weight, precision=TOP_PRECISION) + layer_bias
    negative = jnp.minimum(pre_act, 0.0)
    layer_out = jnp.where(pre_act > 0, pre_act, jnp.expm1(negative))
    grad_pre = cotangent * jnp.where(pre_act > 0, 1.0, jnp.exp(negative))
    grad_scale = 1.0 / math.sqrt(row_count * cycle_size)
    grad_weight = (
        jnp.einsum("rd,re->de", aggregated, grad_pre, precision=TOP_PRECISION) * grad_scale
    )
    grad_bias = jnp.sum(grad_pre, axis=0) * grad_scale
    grad_weight, grad_bias = lax.psum((grad_weight, grad_bias), ("blk", "rep"))
    grad_hidden = jnp.einsum("re,de->rd", grad_pre, weight, precision=TOP_PRECISION)
    hidden_gradient = lax.all_gather(grad_hidden, "rep", axis=0, tiled=True)
    slot_terms = jnp.einsum(
        "xszt,xzc->xstc",
        operator_tiles,
        reshape_to_blocks(hidden_gradient),
        precision=TOP_PRECISION,
    )
    sorted_terms = jnp.einsum("iksc,ikbd->scbd", chosen, slot_terms, precision=TOP_PRECISION)

    def adjoint_term(section_no):
        return lax.dynamic_index_in_dim(sorted_terms, section_no, 0, keepdims=False).reshape(
            row_count, width
        )

    def retreat(counter, running):
        moved = shifted_2(running, "blk", -1)
        return moved + adjoint_term(window - 1 - counter)

    adjoint = lax.fori_loop(1, window, retreat, adjoint_term(window - 1))
    for bit_pos in range(rep_size.bit_length() - 1):
        returned = shifted_2(adjoint, "blk", -(window << bit_pos))
        adjoint = jnp.where((replica >> bit_pos) % 2 == 1, returned, adjoint)
    grad_feats = lax.psum_scatter(adjoint, "rep", scatter_dimension=0, tiled=True)
    return (layer_out, grad_feats, grad_weight, grad_bias)


F32, BF16 = jnp.float32, jnp.bfloat16
HALVES = 2


def split(value):
    high = value.astype(BF16)
    return high, (value - high.astype(F32)).astype(BF16)


def dot3(a, b):
    def product(x, y):
        return jnp.dot(x, y, preferred_element_type=F32)

    return product(a[0], b[0]) + (product(a[0], b[1]) + product(a[1], b[0]))


def kernel(
    n, m, feats, tiles_hbm, cols_hbm, weight_hbm, bias_hbm, cot_hbm,
    out, gfeats, gweight, gbias,
    tiles, cols, weight, bias, cot,
    xs, s_hi, s_lo, st_hi, st_lo, hpart, hrecv, grad, adj, fold, extra, total, frecv,
    gws, gwr, gwz, gfin, send_sem, recv_sem, load_sem,
):
    p, r = lax.axis_index("blk"), lax.axis_index("rep")
    blocks, slots, size, _ = tiles.shape
    rows = blocks * size
    part, width = cot.shape
    cw = width // HALVES
    piece = width // n
    kind = lax.rem(p, 4)
    even = lax.rem(p, 2) == 0
    odd = jnp.logical_not(even)
    moved = r > 0
    always = None

    def both(x, y):
        return jnp.logical_and(x, y)

    def but(x, y):
        return jnp.logical_and(x, jnp.logical_not(y))

    def when(cond, action):
        if cond is None:
            action()
        else:
            pl.when(cond)(action)

    near_from = both(r == 1, kind == 2)
    near_to = both(r == 1, kind == 1)
    above = both(r == 3, kind == 3)
    below = both(r == 2, kind == 2)
    nxt = lax.rem(p + 1, n)
    prv = lax.rem(p - 1 + n, n)

    pairs = [
        (tiles_hbm, tiles),
        (cols_hbm, cols),
        (weight_hbm, weight),
        (bias_hbm, bias),
        (cot_hbm, cot),
    ]
    loads = [
        pltpu.make_async_copy(src, dst, load_sem.at[i]) for i, (src, dst) in enumerate(pairs)
    ]
    for made in loads:
        made.start()

    barrier = pltpu.get_barrier_semaphore()
    for d in range(1, n):
        pl.semaphore_signal(barrier, inc=1, device_id={"blk": lax.rem(p + d, n), "rep": r})
    for d in range(1, m):
        pl.semaphore_signal(barrier, inc=1, device_id={"blk": p, "rep": lax.rem(r + d, m)})

    @pl.when(above)
    def _():
        pl.semaphore_signal(barrier, inc=1, device_id={"blk": prv, "rep": 2})

    @pl.when(below)
    def _():
        pl.semaphore_signal(barrier, inc=1, device_id={"blk": nxt, "rep": 3})

    pl.semaphore_wait(barrier, n + m - 2 + jnp.where(jnp.logical_or(above, below), 1, 0))

    keys, started = {}, []

    def copy(name, src, dst, blk, rep):
        key = keys.setdefault(name, len(keys))
        return pltpu.make_async_remote_copy(
            src_ref=src,
            dst_ref=dst,
            send_sem=send_sem.at[key],
            recv_sem=recv_sem.at[key],
            device_id={"blk": blk, "rep": rep},
        )

    def start(made, cond=always):
        started.append((made, cond))
        when(cond, made.start)

    def half(c):
        return pl.ds(c * cw, cw)

    ahead = lax.rem(p + 2 * r, n)
    after = lax.rem(p + 2 * r + 1, n)
    to_ahead = but(moved, both(r == 1, lax.rem(ahead, 4) == 1))
    to_after = but(odd, both(r == 2, lax.rem(after, 4) == 2))

    def to_first(c, src, blk, rep):
        return copy(("a", c), src, xs.at[0, c], blk, rep)

    def to_second(c, src, blk, rep):
        return copy(("b", c), src, xs.at[1, c], blk, rep)

    def send_features(c):
        start(to_second(c, feats.at[:, half(c)], after, r), to_after)
        start(to_first(c, feats.at[:, half(c)], ahead, r), to_ahead)

    send_features(0)
    features_out = list(started)
    started.clear()
    own = [
        pltpu.make_async_copy(feats.at[:, half(c)], xs.at[0, c], load_sem.at[len(pairs) + c])
        for c in range(HALVES)
    ]

    @pl.when(r == 0)
    def _():
        for c in range(HALVES):
            own[c].start()

    for made in loads:
        made.wait()
    for s in range(2):
        if s == 1:
            for made, cond in features_out:
                when(cond, made.wait_send)
            send_features(1)
        owner = lax.rem(p - 2 * r - s + 2 * n, n)
        for b in range(blocks):
            name = owner * blocks + b
            at = slice((s * blocks + b) * size, (s * blocks + b + 1) * size)
            for i in range(blocks):
                tile = jnp.zeros((size, size), F32)
                for k in range(slots):
                    tile = tile + tiles[i, k] * jnp.where(cols[i, k] == name, 1.0, 0.0)
                high, low = split(tile)
                s_hi[i * size : (i + 1) * size, at] = high
                s_lo[i * size : (i + 1) * size, at] = low
                high, low = split(tile.T)
                st_hi[at, i * size : (i + 1) * size] = high
                st_lo[at, i * size : (i + 1) * size] = low

    def take_first(c):
        @pl.when(moved)
        def _():
            to_first(c, xs.at[0, c], p, r).wait_recv()

        @pl.when(r == 0)
        def _():
            own[c].wait()

        start(to_second(c, xs.at[0, c], nxt, r), even)
        start(to_second(c, xs.at[0, c], prv, r - 1), above)

    def product(c, s):
        at = slice(s * rows, (s + 1) * rows)
        return dot3((s_hi[:, at], s_lo[:, at]), split(xs[s, c]))

    hsends = []

    def aggregate_sends(c):
        made_c = []
        for d in range(m - 1, 0, -1):
            to = lax.rem(r + d, m)
            made = copy(("c", c, d), hpart.at[c, to], hrecv.at[c, d - 1], p, to)
            start(made)
            made_c.append(made)
        hsends.append(made_c)

    for c in range(HALVES):
        @pl.when(near_from)
        def _():
            to_second(c, xs.at[1, c], p, r).wait_recv()
            to_first(c, xs.at[1, c], prv, r).start()

        take_first(c)
        acc = product(c, 0)
        pl.when(jnp.logical_not(near_from))(to_second(c, xs.at[1, c], p, r).wait_recv)
        acc = acc + product(c, 1)
        hpart[c] = acc.reshape(m, part, cw)
        aggregate_sends(c)
    for c in range(HALVES):
        started.append((to_first(c, xs.at[1, c], prv, r), near_from))
    w = split(weight[...])
    wt = split(weight[...].T)
    pre = bias[...]
    parts = []
    for c in range(HALVES):
        for made in hsends[c]:
            made.wait_recv()
        parts.append(hpart[c, r] + ((hrecv[c, 0] + hrecv[c, 1]) + hrecv[c, 2]))
        inner = slice(c * cw, (c + 1) * cw)
        pre = pre + dot3(split(parts[c]), (w[0][inner], w[1][inner]))
    agg = jnp.concatenate(parts, axis=1)

    exped = jnp.exp(jnp.minimum(pre, 0.0))
    gpre = cot[...] * jnp.where(pre > 0, 1.0, exped)
    gpre_parts = split(gpre)
    gsends = []

    def hidden_sends(c):
        made_c = []
        for d in range(m - 1, 0, -1):
            to = lax.rem(r + d, m)
            made = copy(("d", c, d), grad.at[c, r], grad.at[c, r], p, to)
            made.start()
            made_c.append(made)
        gsends.append(made_c)

    for c in range(HALVES):
        columns = slice(c * cw, (c + 1) * cw)
        grad[c, r] = dot3(gpre_parts, (wt[0][:, columns], wt[1][:, columns]))
        if c == 0:
            hidden_sends(0)
    out[...] = jnp.where(pre > 0, pre, exped - 1.0)

    gw = dot3(split(agg.T), gpre_parts)
    gb = jnp.broadcast_to(jnp.sum(gpre, axis=0, keepdims=True), (8, width))
    for q in range(n):
        gws[q, :piece] = gw[q * piece : (q + 1) * piece]
        gws[q, piece:] = gb
    gwr[p] = gws[p]
    esends = []
    for d in range(1, n):
        to = lax.rem(p + d, n)
        made = copy(("e", d), gws.at[to], gwr.at[p], to, r)
        start(made)
        esends.append(made)

    def weight_sums():
        for made in esends:
            made.wait_recv()
        total_p = gwr[0]
        for q in range(1, n):
            total_p = total_p + gwr[q]
        gwz[r] = total_p
        made_z = []
        for d in range(m - 1, 0, -1):
            to = lax.rem(r + d, m)
            made = copy(("m", d), gwz.at[r], gwz.at[r], p, to)
            start(made)
            made_z.append(made)
        return made_z

    scale = 1.0 / math.sqrt(rows * n)

    def weight_gather(made_z):
        for made in made_z:
            made.wait_recv()
        whole = gwz[0]
        for q in range(1, m):
            whole = whole + gwz[q]
        gfin[p] = whole[:piece] * scale
        gbias[...] = whole[piece : piece + 1] * scale
        made_n = []
        for d in range(1, n):
            to = lax.rem(p + d, n)
            made = copy(("n", d), gfin.at[p], gfin.at[p], to, r)
            start(made)
            made_n.append(made)
        return made_n

    back = lax.rem(p - 2 * r + n, n)
    before = lax.rem(p - 2 * r - 1 + 2 * n, n)
    order = [m - 1 - j for j in range(m)]

    def place(d):
        return lax.rem(r + d, m)

    def to_fold(c, d, blk):
        b = place(d)
        return copy(("f", c, d), adj.at[1, c, b], fold.at[c, b], blk, r)

    def to_near(c, d):
        b = place(d)
        return copy(("g", c, d), adj.at[0, c, b], extra.at[c, b], nxt, r)

    def to_above(c, b):
        return copy(("h", c, b), adj.at[1, c, b], extra.at[c, b], nxt, r + 1)

    def to_total(c, d):
        b = place(d)
        return copy(("k", c, d), adj.at[0, c, b], total.at[c, b], back, r)

    plain_second = but(but(even, below), near_from)
    plain_first = but(but(both(odd, moved), near_to), above)

    def adjoint(c):
        for made in gsends[c]:
            made.wait_recv()
        g = split(grad[c].reshape(rows, cw))
        adj[1, c] = dot3((st_hi[rows:], st_lo[rows:]), g).reshape(m, part, cw)
        for d in order:
            start(to_fold(c, d, prv), odd)
            start(to_fold(c, d, before), plain_second)
        for b in range(m):
            start(to_above(c, b), below)
        adj[0, c] = dot3((st_hi[:rows], st_lo[:rows]), g).reshape(m, part, cw)
        for d in order:
            start(to_near(c, d), near_to)
            start(to_total(c, d), plain_first)

        @pl.when(even)
        def _():
            for d in order:
                b = place(d)
                to_fold(c, d, prv).wait_recv()
                adj[0, c, b] = adj[0, c, b] + fold[c, b]
                pl.when(moved)(to_total(c, d).start)

        @pl.when(above)
        def _():
            for d in order:
                b = (3 + d) % m
                to_above(c, b).wait_recv()
                adj[0, c, b] = adj[0, c, b] + extra[c, b]
                to_total(c, d).start()

        @pl.when(near_from)
        def _():
            for d in order:
                b = place(d)
                to_near(c, d).wait_recv()
                adj[1, c, b] = adj[1, c, b] + extra[c, b]
                to_fold(c, d, before).start()

        for d in order:
            started.append((to_total(c, d), both(even, moved)))
            started.append((to_total(c, d), above))
            started.append((to_fold(c, d, before), near_from))

    from_total = but(moved, both(r == 1, kind == 3))
    from_fold = but(odd, both(r == 2, kind == 1))

    def adjoint_reduce(c):
        made_c = []
        for d in order:
            b = place(d)

            @pl.when(from_total)
            def _():
                to_total(c, d).wait_recv()

            @pl.when(r == 0)
            def _():
                total[c, b] = adj[0, c, b]

            @pl.when(from_fold)
            def _():
                to_fold(c, d, prv).wait_recv()

                @pl.when(from_total)
                def _():
                    total[c, b] = total[c, b] + fold[c, b]

                @pl.when(r == 0)
                def _():
                    total[c, b] = total[c, b] + fold[c, b]

                @pl.when(both(r == 1, kind == 3))
                def _():
                    total[c, b] = fold[c, b]

            if d:
                made = copy(("l", c, d), total.at[c, b], frecv.at[c, d - 1], p, b)
                start(made)
                made_c.append(made)
        return made_c

    for made in gsends[0]:
        made.wait_send()
    hidden_sends(1)
    for made in gsends[1]:
        started.append((made, always))
    adjoint(0)
    made_z = weight_sums()
    adjoint(1)
    lsends = [adjoint_reduce(0)]
    made_n = weight_gather(made_z)
    lsends.append(adjoint_reduce(1))
    for c in range(HALVES):
        if c == 1:
            for made in made_n:
                made.wait_recv()
            gweight[...] = gfin[...].reshape(width, width)
        for made in lsends[c]:
            made.wait_recv()
        gfeats[:, half(c)] = total[c, r] + ((frecv[c, 0] + frecv[c, 1]) + frecv[c, 2])
    for made, cond in started:
        when(cond, made.wait_send)


def store_results(*refs):
    count = len(refs) // 2
    sems = refs[-1]
    copies = [pltpu.make_async_copy(refs[i], refs[count + i], sems.at[i]) for i in range(count)]
    for made in copies:
        made.start()
    for made in copies:
        made.wait()


def fast_body(n, m, node_feats, operator_tiles, tile_cols, weight, layer_bias, cotangent):
    blocks, _, size, _ = operator_tiles.shape
    rows = blocks * size
    part, width = cotangent.shape
    cw = width // HALVES
    piece = width // n
    copies = HALVES * (2 + 3 * (m - 1) + 4 * m) + 2 * (n - 1) + (m - 1)
    vmem = pl.BlockSpec(memory_space=pltpu.VMEM)
    shape = jax.ShapeDtypeStruct
    quarter = (HALVES, m, part, cw)
    result = pl.pallas_call(
        functools.partial(kernel, n, m),
        out_shape=(
            shape((part, width), F32),
            shape((part, width), F32),
            shape((width, width), F32),
            shape((1, width), F32),
        ),
        in_specs=[pl.BlockSpec(memory_space=pltpu.HBM)] * 6,
        out_specs=(vmem,) * 4,
        scratch_shapes=[
            pltpu.VMEM(operator_tiles.shape, F32),
            pltpu.SMEM(tile_cols.shape, jnp.int32),
            pltpu.VMEM((width, width), F32),
            pltpu.VMEM((1, width), F32),
            pltpu.VMEM((part, width), F32),
            pltpu.VMEM((2, HALVES, rows, cw), F32),
            pltpu.VMEM((rows, 2 * rows), BF16),
            pltpu.VMEM((rows, 2 * rows), BF16),
            pltpu.VMEM((2 * rows, rows), BF16),
            pltpu.VMEM((2 * rows, rows), BF16),
            pltpu.VMEM(quarter, F32),
            pltpu.VMEM((HALVES, m - 1, part, cw), F32),
            pltpu.VMEM(quarter, F32),
            pltpu.VMEM((2,) + quarter, F32),
            pltpu.VMEM(quarter, F32),
            pltpu.VMEM(quarter, F32),
            pltpu.VMEM(quarter, F32),
            pltpu.VMEM((HALVES, m - 1, part, cw), F32),
            pltpu.VMEM((n, piece + 8, width), F32),
            pltpu.VMEM((n, piece + 8, width), F32),
            pltpu.VMEM((m, piece + 8, width), F32),
            pltpu.VMEM((n, piece, width), F32),
            pltpu.SemaphoreType.DMA((copies,)),
            pltpu.SemaphoreType.DMA((copies,)),
            pltpu.SemaphoreType.DMA((5 + HALVES,)),
        ],
        compiler_params=pltpu.CompilerParams(
            collective_id=0, has_side_effects=True, vmem_limit_bytes=63 * 1024 * 1024
        ),
    )(node_feats, operator_tiles, tile_cols, weight, layer_bias.reshape(1, width), cotangent)
    layer_out, grad_feats, grad_weight, grad_bias = pl.pallas_call(
        store_results,
        out_shape=[shape(value.shape, F32) for value in result],
        in_specs=[pl.BlockSpec(memory_space=pl.ANY)] * len(result),
        out_specs=[pl.BlockSpec(memory_space=pl.ANY)] * len(result),
        scratch_shapes=[pltpu.SemaphoreType.DMA((len(result),))],
    )(*result)
    return layer_out, grad_feats, grad_weight, grad_bias.reshape(width)


def solution(mesh):
    n, m = mesh.shape["blk"], mesh.shape["rep"]
    fits = n == 2 * m and m == 4
    return jax.shard_map(
        functools.partial(fast_body, n, m) if fits else body,
        mesh=mesh,
        in_specs=(
            P("blk", None),
            P("blk", "rep", None, None),
            P("blk", "rep"),
            P(),
            P(),
            P(("blk", "rep"), None),
        ),
        out_specs=(P(("blk", "rep"), None), P(("blk", "rep"), None), P(), P()),
        check_vma=False,
    )
```

```python
import functools
import math

import jax
import jax.numpy as jnp
from jax import lax
from jax.experimental import pallas as pl
from jax.experimental.pallas import tpu as pltpu
from jax.sharding import PartitionSpec as P

TOP_PRECISION = lax.Precision.HIGHEST


def shifted_2(value, axis, steps):
    count = lax.axis_size(axis)
    pairs = [(source, (source + steps) % count) for source in range(count)]
    return lax.ppermute(value, axis, pairs)


def body(node_feats, operator_tiles, tile_cols, weight, layer_bias, cotangent):
    cycle_size = lax.axis_size("blk")
    rep_size = lax.axis_size("rep")
    window = cycle_size // rep_size
    position = lax.axis_index("blk")
    replica = lax.axis_index("rep")
    offset = replica * window
    blocks, slot_count, tile_size, _ = operator_tiles.shape
    width = node_feats.shape[1]
    row_count = blocks * tile_size
    owners = tile_cols // blocks
    within = tile_cols % blocks
    distance = jnp.mod(position - owners, cycle_size) - offset
    columns = jnp.arange(blocks, dtype=jnp.int32)
    sections = jnp.arange(window, dtype=jnp.int32)
    chosen = (
        (distance[:, :, None, None] == sections[None, None, :, None])
        & (within[:, :, None, None] == columns[None, None, None, :])
    ).astype(jnp.float32)

    def reshape_to_blocks(rows):
        return rows.reshape(blocks, tile_size, width)

    def store(stacked, section_no, current):
        return lax.dynamic_update_index_in_dim(stacked, reshape_to_blocks(current), section_no, 0)

    aligned = node_feats
    for bit_pos in range(rep_size.bit_length() - 1):
        shifted = shifted_2(aligned, "blk", window << bit_pos)
        aligned = jnp.where((replica >> bit_pos) % 2 == 1, shifted, aligned)
    empty = jnp.zeros((window, blocks, tile_size, width), jnp.float32)

    def advance(section_no, loop_state):
        current, stacked = loop_state
        current = shifted_2(current, "blk", 1)
        return (current, store(stacked, section_no, current))

    _, received = lax.fori_loop(1, window, advance, (aligned, store(empty, 0, aligned)))
    selected_tiles = jnp.einsum("iksc,scbd->ikbd", chosen, received, precision=TOP_PRECISION)
    partial_aggregate = jnp.einsum(
        "uzrj,uzje->ure", operator_tiles, selected_tiles, precision=TOP_PRECISION
    ).reshape(row_count, width)
    aggregated = lax.psum_scatter(partial_aggregate, "rep", scatter_dimension=0, tiled=True)
    pre_act = jnp.dot(aggregated, weight, precision=TOP_PRECISION) + layer_bias
    negative = jnp.minimum(pre_act, 0.0)
    layer_out = jnp.where(pre_act > 0, pre_act, jnp.expm1(negative))
    grad_pre = cotangent * jnp.where(pre_act > 0, 1.0, jnp.exp(negative))
    grad_scale = 1.0 / math.sqrt(row_count * cycle_size)
    grad_weight = (
        jnp.einsum("rd,re->de", aggregated, grad_pre, precision=TOP_PRECISION) * grad_scale
    )
    grad_bias = jnp.sum(grad_pre, axis=0) * grad_scale
    grad_weight, grad_bias = lax.psum((grad_weight, grad_bias), ("blk", "rep"))
    grad_hidden = jnp.einsum("re,de->rd", grad_pre, weight, precision=TOP_PRECISION)
    hidden_gradient = lax.all_gather(grad_hidden, "rep", axis=0, tiled=True)
    slot_terms = jnp.einsum(
        "xszt,xzc->xstc",
        operator_tiles,
        reshape_to_blocks(hidden_gradient),
        precision=TOP_PRECISION,
    )
    sorted_terms = jnp.einsum("iksc,ikbd->scbd", chosen, slot_terms, precision=TOP_PRECISION)

    def adjoint_term(section_no):
        return lax.dynamic_index_in_dim(sorted_terms, section_no, 0, keepdims=False).reshape(
            row_count, width
        )

    def retreat(counter, running):
        moved = shifted_2(running, "blk", -1)
        return moved + adjoint_term(window - 1 - counter)

    adjoint = lax.fori_loop(1, window, retreat, adjoint_term(window - 1))
    for bit_pos in range(rep_size.bit_length() - 1):
        returned = shifted_2(adjoint, "blk", -(window << bit_pos))
        adjoint = jnp.where((replica >> bit_pos) % 2 == 1, returned, adjoint)
    grad_feats = lax.psum_scatter(adjoint, "rep", scatter_dimension=0, tiled=True)
    return (layer_out, grad_feats, grad_weight, grad_bias)


F32, BF16 = jnp.float32, jnp.bfloat16
HALVES = 2


def split(value):
    high = value.astype(BF16)
    return high, (value - high.astype(F32)).astype(BF16)


def dot3(a, b):
    def product(x, y):
        return jnp.dot(x, y, preferred_element_type=F32)

    return product(a[0], b[0]) + (product(a[0], b[1]) + product(a[1], b[0]))


def kernel(
    n, m, feats, tiles_hbm, cols_hbm, weight_hbm, bias_hbm, cot_hbm,
    out, gfeats, gweight, gbias,
    tiles, cols, weight, bias, cot,
    xs, s_hi, s_lo, st_hi, st_lo, hpart, hrecv, grad, adj, fold, extra, total, frecv,
    gws, gwr, gwz, gfin, send_sem, recv_sem, load_sem,
):
    p, r = lax.axis_index("blk"), lax.axis_index("rep")
    blocks, slots, size, _ = tiles.shape
    rows = blocks * size
    part, width = cot.shape
    cw = width // HALVES
    piece = width // n
    kind = lax.rem(p, 4)
    even = lax.rem(p, 2) == 0
    odd = jnp.logical_not(even)
    moved = r > 0
    always = None

    def both(x, y):
        return jnp.logical_and(x, y)

    def but(x, y):
        return jnp.logical_and(x, jnp.logical_not(y))

    def when(cond, action):
        if cond is None:
            action()
        else:
            pl.when(cond)(action)

    near_from = both(r == 1, kind == 2)
    near_to = both(r == 1, kind == 1)
    above = both(r == 3, kind == 3)
    below = both(r == 2, kind == 2)
    nxt = lax.rem(p + 1, n)
    prv = lax.rem(p - 1 + n, n)

    pairs = [
        (tiles_hbm, tiles),
        (cols_hbm, cols),
        (weight_hbm, weight),
        (bias_hbm, bias),
        (cot_hbm, cot),
    ]
    loads = [
        pltpu.make_async_copy(src, dst, load_sem.at[i]) for i, (src, dst) in enumerate(pairs)
    ]
    for made in loads:
        made.start()

    barrier = pltpu.get_barrier_semaphore()
    for d in range(1, n):
        pl.semaphore_signal(barrier, inc=1, device_id={"blk": lax.rem(p + d, n), "rep": r})
    for d in range(1, m):
        pl.semaphore_signal(barrier, inc=1, device_id={"blk": p, "rep": lax.rem(r + d, m)})

    @pl.when(above)
    def _():
        pl.semaphore_signal(barrier, inc=1, device_id={"blk": prv, "rep": 2})

    @pl.when(below)
    def _():
        pl.semaphore_signal(barrier, inc=1, device_id={"blk": nxt, "rep": 3})

    pl.semaphore_wait(barrier, n + m - 2 + jnp.where(jnp.logical_or(above, below), 1, 0))

    keys, started = {}, []

    def copy(name, src, dst, blk, rep):
        key = keys.setdefault(name, len(keys))
        return pltpu.make_async_remote_copy(
            src_ref=src,
            dst_ref=dst,
            send_sem=send_sem.at[key],
            recv_sem=recv_sem.at[key],
            device_id={"blk": blk, "rep": rep},
        )

    def start(made, cond=always):
        started.append((made, cond))
        when(cond, made.start)

    def flush():
        for made, cond in started:
            when(cond, made.wait_send)
        started.clear()

    def half(c):
        return pl.ds(c * cw, cw)

    ahead = lax.rem(p + 2 * r, n)
    after = lax.rem(p + 2 * r + 1, n)
    to_ahead, to_after = moved, odd

    def to_first(c, src, blk, rep):
        return copy(("a", c), src, xs.at[0, c], blk, rep)

    def to_second(c, src, blk, rep):
        return copy(("b", c), src, xs.at[1, c], blk, rep)

    def send_features(c):
        start(to_second(c, feats.at[:, half(c)], after, r), to_after)
        start(to_first(c, feats.at[:, half(c)], ahead, r), to_ahead)

    send_features(0)
    own = [
        pltpu.make_async_copy(feats.at[:, half(c)], xs.at[0, c], load_sem.at[len(pairs) + c])
        for c in range(HALVES)
    ]

    @pl.when(r == 0)
    def _():
        for c in range(HALVES):
            own[c].start()

    for made in loads:
        made.wait()
    for s in range(2):
        if s == 1:
            flush()
            send_features(1)
        owner = lax.rem(p - 2 * r - s + 2 * n, n)
        for b in range(blocks):
            name = owner * blocks + b
            at = slice((s * blocks + b) * size, (s * blocks + b + 1) * size)
            for i in range(blocks):
                tile = jnp.zeros((size, size), F32)
                for k in range(slots):
                    tile = tile + tiles[i, k] * jnp.where(cols[i, k] == name, 1.0, 0.0)
                high, low = split(tile)
                s_hi[i * size : (i + 1) * size, at] = high
                s_lo[i * size : (i + 1) * size, at] = low
                high, low = split(tile.T)
                st_hi[at, i * size : (i + 1) * size] = high
                st_lo[at, i * size : (i + 1) * size] = low

    def take_first(c):
        @pl.when(moved)
        def _():
            to_first(c, xs.at[0, c], p, r).wait_recv()

        @pl.when(r == 0)
        def _():
            own[c].wait()

        start(to_second(c, xs.at[0, c], nxt, r), even)

    def product(c, s):
        at = slice(s * rows, (s + 1) * rows)
        return dot3((s_hi[:, at], s_lo[:, at]), split(xs[s, c]))

    hsends = []

    def aggregate_sends(c):
        made_c = []
        for d in range(m - 1, 0, -1):
            to = lax.rem(r + d, m)
            made = copy(("c", c, d), hpart.at[c, to], hrecv.at[c, d - 1], p, to)
            start(made)
            made_c.append(made)
        hsends.append(made_c)

    for c in range(HALVES):
        take_first(c)
        acc = product(c, 0)
        to_second(c, xs.at[1, c], p, r).wait_recv()
        acc = acc + product(c, 1)
        hpart[c] = acc.reshape(m, part, cw)
        aggregate_sends(c)
    w = split(weight[...])
    wt = split(weight[...].T)
    pre = bias[...]
    parts = []
    for c in range(HALVES):
        for made in hsends[c]:
            made.wait_recv()
        parts.append(hpart[c, r] + ((hrecv[c, 0] + hrecv[c, 1]) + hrecv[c, 2]))
        inner = slice(c * cw, (c + 1) * cw)
        pre = pre + dot3(split(parts[c]), (w[0][inner], w[1][inner]))
    agg = jnp.concatenate(parts, axis=1)

    exped = jnp.exp(jnp.minimum(pre, 0.0))
    gpre = cot[...] * jnp.where(pre > 0, 1.0, exped)
    gpre_parts = split(gpre)
    gsends = []

    def hidden_sends(c):
        made_c = []
        for d in range(m - 1, 0, -1):
            to = lax.rem(r + d, m)
            made = copy(("d", c, d), grad.at[c, r], grad.at[c, r], p, to)
            made.start()
            made_c.append(made)
        gsends.append(made_c)

    for c in range(HALVES):
        columns = slice(c * cw, (c + 1) * cw)
        grad[c, r] = dot3(gpre_parts, (wt[0][:, columns], wt[1][:, columns]))
        if c == 0:
            hidden_sends(0)
    out[...] = jnp.where(pre > 0, pre, exped - 1.0)

    gw = dot3(split(agg.T), gpre_parts)
    gb = jnp.broadcast_to(jnp.sum(gpre, axis=0, keepdims=True), (8, width))
    for q in range(n):
        gws[q, :piece] = gw[q * piece : (q + 1) * piece]
        gws[q, piece:] = gb
    gwr[p] = gws[p]
    esends = []
    for d in range(1, n):
        to = lax.rem(p + d, n)
        made = copy(("e", d), gws.at[to], gwr.at[p], to, r)
        start(made)
        esends.append(made)

    def weight_sums():
        for made in esends:
            made.wait_recv()
        total_p = gwr[0]
        for q in range(1, n):
            total_p = total_p + gwr[q]
        gwz[r] = total_p
        made_z = []
        for d in range(m - 1, 0, -1):
            to = lax.rem(r + d, m)
            made = copy(("m", d), gwz.at[r], gwz.at[r], p, to)
            start(made)
            made_z.append(made)
        return made_z

    scale = 1.0 / math.sqrt(rows * n)

    def weight_gather(made_z):
        for made in made_z:
            made.wait_recv()
        whole = gwz[0]
        for q in range(1, m):
            whole = whole + gwz[q]
        gfin[p] = whole[:piece] * scale
        gbias[...] = whole[piece : piece + 1] * scale
        made_n = []
        for d in range(1, n):
            to = lax.rem(p + d, n)
            made = copy(("n", d), gfin.at[p], gfin.at[p], to, r)
            start(made)
            made_n.append(made)
        return made_n

    back = lax.rem(p - 2 * r + n, n)
    before = lax.rem(p - 2 * r - 1 + 2 * n, n)
    order = [m - 1 - j for j in range(m)]

    def place(d):
        return lax.rem(r + d, m)

    def to_fold(c, d, blk):
        b = place(d)
        return copy(("f", c, d), adj.at[1, c, b], fold.at[c, b], blk, r)

    def to_near(c, d):
        b = place(d)
        return copy(("g", c, d), adj.at[0, c, b], extra.at[c, b], nxt, r)

    def to_above(c, b):
        return copy(("h", c, b), adj.at[1, c, b], extra.at[c, b], nxt, r + 1)

    def to_total(c, d):
        b = place(d)
        return copy(("k", c, d), adj.at[0, c, b], total.at[c, b], back, r)

    plain_second = but(but(even, below), near_from)
    plain_first = but(but(both(odd, moved), near_to), above)

    def adjoint(c):
        for made in gsends[c]:
            made.wait_recv()
        g = split(grad[c].reshape(rows, cw))
        adj[1, c] = dot3((st_hi[rows:], st_lo[rows:]), g).reshape(m, part, cw)
        for d in order:
            start(to_fold(c, d, prv), odd)
            start(to_fold(c, d, before), plain_second)
        for b in range(m):
            start(to_above(c, b), below)
        adj[0, c] = dot3((st_hi[:rows], st_lo[:rows]), g).reshape(m, part, cw)
        for d in order:
            start(to_near(c, d), near_to)
            start(to_total(c, d), plain_first)

        @pl.when(even)
        def _():
            for d in order:
                b = place(d)
                to_fold(c, d, prv).wait_recv()
                adj[0, c, b] = adj[0, c, b] + fold[c, b]
                pl.when(moved)(to_total(c, d).start)

        @pl.when(above)
        def _():
            for d in order:
                b = (3 + d) % m
                to_above(c, b).wait_recv()
                adj[0, c, b] = adj[0, c, b] + extra[c, b]
                to_total(c, d).start()

        @pl.when(near_from)
        def _():
            for d in order:
                b = place(d)
                to_near(c, d).wait_recv()
                adj[1, c, b] = adj[1, c, b] + extra[c, b]
                to_fold(c, d, before).start()

        for d in order:
            started.append((to_total(c, d), both(even, moved)))
            started.append((to_total(c, d), above))
            started.append((to_fold(c, d, before), near_from))

    from_total = but(moved, both(r == 1, kind == 3))
    from_fold = but(odd, both(r == 2, kind == 1))

    def adjoint_reduce(c):
        made_c = []
        for d in order:
            b = place(d)

            @pl.when(from_total)
            def _():
                to_total(c, d).wait_recv()

            @pl.when(r == 0)
            def _():
                total[c, b] = adj[0, c, b]

            @pl.when(from_fold)
            def _():
                to_fold(c, d, prv).wait_recv()

                @pl.when(from_total)
                def _():
                    total[c, b] = total[c, b] + fold[c, b]

                @pl.when(r == 0)
                def _():
                    total[c, b] = total[c, b] + fold[c, b]

                @pl.when(both(r == 1, kind == 3))
                def _():
                    total[c, b] = fold[c, b]

            if d:
                made = copy(("l", c, d), total.at[c, b], frecv.at[c, d - 1], p, b)
                start(made)
                made_c.append(made)
        return made_c

    for made in gsends[0]:
        made.wait_send()
    hidden_sends(1)
    flush()
    for made in gsends[1]:
        started.append((made, always))
    adjoint(0)
    made_z = weight_sums()
    adjoint(1)
    lsends = [adjoint_reduce(0)]
    made_n = weight_gather(made_z)
    lsends.append(adjoint_reduce(1))
    flush()
    for c in range(HALVES):
        if c == 1:
            for made in made_n:
                made.wait_recv()
            gweight[...] = gfin[...].reshape(width, width)
        for made in lsends[c]:
            made.wait_recv()
        gfeats[:, half(c)] = total[c, r] + ((frecv[c, 0] + frecv[c, 1]) + frecv[c, 2])
    flush()


def store_results(*refs):
    count = len(refs) // 3
    sources, targets, stages = refs[:count], refs[count : 2 * count], refs[2 * count : 3 * count]
    sems = refs[-1]
    loads = [
        pltpu.make_async_copy(sources[i], stages[i], sems.at[0, i]) for i in range(count)
    ]
    stores = [
        pltpu.make_async_copy(stages[i], targets[i], sems.at[1, i]) for i in range(count)
    ]
    for made in loads:
        made.start()
    for load, store in zip(loads, stores):
        load.wait()
        store.start()
    for made in stores:
        made.wait()


def fast_body(n, m, node_feats, operator_tiles, tile_cols, weight, layer_bias, cotangent):
    blocks, _, size, _ = operator_tiles.shape
    rows = blocks * size
    part, width = cotangent.shape
    cw = width // HALVES
    piece = width // n
    copies = HALVES * (2 + 3 * (m - 1) + 4 * m) + 2 * (n - 1) + (m - 1)
    vmem = pl.BlockSpec(memory_space=pltpu.VMEM)
    shape = jax.ShapeDtypeStruct
    quarter = (HALVES, m, part, cw)
    result = pl.pallas_call(
        functools.partial(kernel, n, m),
        out_shape=(
            shape((part, width), F32),
            shape((part, width), F32),
            shape((width, width), F32),
            shape((1, width), F32),
        ),
        in_specs=[pl.BlockSpec(memory_space=pltpu.HBM)] * 6,
        out_specs=(vmem,) * 4,
        scratch_shapes=[
            pltpu.VMEM(operator_tiles.shape, F32),
            pltpu.SMEM(tile_cols.shape, jnp.int32),
            pltpu.VMEM((width, width), F32),
            pltpu.VMEM((1, width), F32),
            pltpu.VMEM((part, width), F32),
            pltpu.VMEM((2, HALVES, rows, cw), F32),
            pltpu.VMEM((rows, 2 * rows), BF16),
            pltpu.VMEM((rows, 2 * rows), BF16),
            pltpu.VMEM((2 * rows, rows), BF16),
            pltpu.VMEM((2 * rows, rows), BF16),
            pltpu.VMEM(quarter, F32),
            pltpu.VMEM((HALVES, m - 1, part, cw), F32),
            pltpu.VMEM(quarter, F32),
            pltpu.VMEM((2,) + quarter, F32),
            pltpu.VMEM(quarter, F32),
            pltpu.VMEM(quarter, F32),
            pltpu.VMEM(quarter, F32),
            pltpu.VMEM((HALVES, m - 1, part, cw), F32),
            pltpu.VMEM((n, piece + 8, width), F32),
            pltpu.VMEM((n, piece + 8, width), F32),
            pltpu.VMEM((m, piece + 8, width), F32),
            pltpu.VMEM((n, piece, width), F32),
            pltpu.SemaphoreType.DMA((copies,)),
            pltpu.SemaphoreType.DMA((copies,)),
            pltpu.SemaphoreType.DMA((5 + HALVES,)),
        ],
        compiler_params=pltpu.CompilerParams(
            collective_id=0, has_side_effects=True, vmem_limit_bytes=63 * 1024 * 1024
        ),
    )(node_feats, operator_tiles, tile_cols, weight, layer_bias.reshape(1, width), cotangent)
    layer_out, grad_feats, grad_weight, grad_bias = pl.pallas_call(
        store_results,
        out_shape=[shape(value.shape, F32) for value in result],
        in_specs=[pl.BlockSpec(memory_space=pl.ANY)] * len(result),
        out_specs=[pl.BlockSpec(memory_space=pl.ANY)] * len(result),
        scratch_shapes=[pltpu.VMEM(value.shape, F32) for value in result]
        + [pltpu.SemaphoreType.DMA((2, len(result)))],
        compiler_params=pltpu.CompilerParams(vmem_limit_bytes=63 * 1024 * 1024),
    )(*result)
    return layer_out, grad_feats, grad_weight, grad_bias.reshape(width)


def solution(mesh):
    n, m = mesh.shape["blk"], mesh.shape["rep"]
    fits = n == 2 * m and m == 4
    return jax.shard_map(
        functools.partial(fast_body, n, m) if fits else body,
        mesh=mesh,
        in_specs=(
            P("blk", None),
            P("blk", "rep", None, None),
            P("blk", "rep"),
            P(),
            P(),
            P(("blk", "rep"), None),
        ),
        out_specs=(P(("blk", "rep"), None), P(("blk", "rep"), None), P(), P()),
        check_vma=False,
    )
```

```python
import functools
import math

import jax
import jax.numpy as jnp
from jax import lax
from jax.experimental import pallas as pl
from jax.experimental.pallas import tpu as pltpu
from jax.sharding import PartitionSpec as P

TOP_PRECISION = lax.Precision.HIGHEST


def shifted_2(value, axis, steps):
    count = lax.axis_size(axis)
    pairs = [(source, (source + steps) % count) for source in range(count)]
    return lax.ppermute(value, axis, pairs)


def body(node_feats, operator_tiles, tile_cols, weight, layer_bias, cotangent):
    cycle_size = lax.axis_size("blk")
    rep_size = lax.axis_size("rep")
    window = cycle_size // rep_size
    position = lax.axis_index("blk")
    replica = lax.axis_index("rep")
    offset = replica * window
    blocks, slot_count, tile_size, _ = operator_tiles.shape
    width = node_feats.shape[1]
    row_count = blocks * tile_size
    owners = tile_cols // blocks
    within = tile_cols % blocks
    distance = jnp.mod(position - owners, cycle_size) - offset
    columns = jnp.arange(blocks, dtype=jnp.int32)
    sections = jnp.arange(window, dtype=jnp.int32)
    chosen = (
        (distance[:, :, None, None] == sections[None, None, :, None])
        & (within[:, :, None, None] == columns[None, None, None, :])
    ).astype(jnp.float32)

    def reshape_to_blocks(rows):
        return rows.reshape(blocks, tile_size, width)

    def store(stacked, section_no, current):
        return lax.dynamic_update_index_in_dim(stacked, reshape_to_blocks(current), section_no, 0)

    aligned = node_feats
    for bit_pos in range(rep_size.bit_length() - 1):
        shifted = shifted_2(aligned, "blk", window << bit_pos)
        aligned = jnp.where((replica >> bit_pos) % 2 == 1, shifted, aligned)
    empty = jnp.zeros((window, blocks, tile_size, width), jnp.float32)

    def advance(section_no, loop_state):
        current, stacked = loop_state
        current = shifted_2(current, "blk", 1)
        return (current, store(stacked, section_no, current))

    _, received = lax.fori_loop(1, window, advance, (aligned, store(empty, 0, aligned)))
    selected_tiles = jnp.einsum("iksc,scbd->ikbd", chosen, received, precision=TOP_PRECISION)
    partial_aggregate = jnp.einsum(
        "uzrj,uzje->ure", operator_tiles, selected_tiles, precision=TOP_PRECISION
    ).reshape(row_count, width)
    aggregated = lax.psum_scatter(partial_aggregate, "rep", scatter_dimension=0, tiled=True)
    pre_act = jnp.dot(aggregated, weight, precision=TOP_PRECISION) + layer_bias
    negative = jnp.minimum(pre_act, 0.0)
    layer_out = jnp.where(pre_act > 0, pre_act, jnp.expm1(negative))
    grad_pre = cotangent * jnp.where(pre_act > 0, 1.0, jnp.exp(negative))
    grad_scale = 1.0 / math.sqrt(row_count * cycle_size)
    grad_weight = (
        jnp.einsum("rd,re->de", aggregated, grad_pre, precision=TOP_PRECISION) * grad_scale
    )
    grad_bias = jnp.sum(grad_pre, axis=0) * grad_scale
    grad_weight, grad_bias = lax.psum((grad_weight, grad_bias), ("blk", "rep"))
    grad_hidden = jnp.einsum("re,de->rd", grad_pre, weight, precision=TOP_PRECISION)
    hidden_gradient = lax.all_gather(grad_hidden, "rep", axis=0, tiled=True)
    slot_terms = jnp.einsum(
        "xszt,xzc->xstc",
        operator_tiles,
        reshape_to_blocks(hidden_gradient),
        precision=TOP_PRECISION,
    )
    sorted_terms = jnp.einsum("iksc,ikbd->scbd", chosen, slot_terms, precision=TOP_PRECISION)

    def adjoint_term(section_no):
        return lax.dynamic_index_in_dim(sorted_terms, section_no, 0, keepdims=False).reshape(
            row_count, width
        )

    def retreat(counter, running):
        moved = shifted_2(running, "blk", -1)
        return moved + adjoint_term(window - 1 - counter)

    adjoint = lax.fori_loop(1, window, retreat, adjoint_term(window - 1))
    for bit_pos in range(rep_size.bit_length() - 1):
        returned = shifted_2(adjoint, "blk", -(window << bit_pos))
        adjoint = jnp.where((replica >> bit_pos) % 2 == 1, returned, adjoint)
    grad_feats = lax.psum_scatter(adjoint, "rep", scatter_dimension=0, tiled=True)
    return (layer_out, grad_feats, grad_weight, grad_bias)


F32, BF16 = jnp.float32, jnp.bfloat16
HALVES = 2
ROW_PARTS = 2


def split(value):
    high = value.astype(BF16)
    return high, (value - high.astype(F32)).astype(BF16)


def dot3(a, b):
    def product(x, y):
        return jnp.dot(x, y, preferred_element_type=F32)

    return product(a[0], b[0]) + (product(a[0], b[1]) + product(a[1], b[0]))


def kernel(
    n, m, feats, tiles_hbm, cols_hbm, weight_hbm, bias_hbm, cot_hbm,
    out, gfeats, gweight, gbias,
    tiles, cols, weight, bias, cot,
    xs, s_hi, s_lo, st_hi, st_lo, hpart, hrecv, grad, adj, fold, extra, total, frecv,
    gws, gwr, gwz, gfin, send_sem, recv_sem, load_sem,
):
    p, r = lax.axis_index("blk"), lax.axis_index("rep")
    blocks, slots, size, _ = tiles.shape
    rows = blocks * size
    part, width = cot.shape
    cw = width // HALVES
    piece = width // n
    kind = lax.rem(p, 4)
    even = lax.rem(p, 2) == 0
    odd = jnp.logical_not(even)
    moved = r > 0
    always = None

    def both(x, y):
        return jnp.logical_and(x, y)

    def but(x, y):
        return jnp.logical_and(x, jnp.logical_not(y))

    def when(cond, action):
        if cond is None:
            action()
        else:
            pl.when(cond)(action)

    near_from = both(r == 1, kind == 2)
    near_to = both(r == 1, kind == 1)
    above = both(r == 3, kind == 3)
    below = both(r == 2, kind == 2)
    nxt = lax.rem(p + 1, n)
    prv = lax.rem(p - 1 + n, n)

    pairs = [
        (tiles_hbm, tiles),
        (cols_hbm, cols),
        (weight_hbm, weight),
        (bias_hbm, bias),
        (cot_hbm, cot),
    ]
    loads = [
        pltpu.make_async_copy(src, dst, load_sem.at[i]) for i, (src, dst) in enumerate(pairs)
    ]
    for made in loads:
        made.start()

    barrier = pltpu.get_barrier_semaphore()
    for d in range(1, n):
        pl.semaphore_signal(barrier, inc=1, device_id={"blk": lax.rem(p + d, n), "rep": r})
    for d in range(1, m):
        pl.semaphore_signal(barrier, inc=1, device_id={"blk": p, "rep": lax.rem(r + d, m)})

    @pl.when(above)
    def _():
        pl.semaphore_signal(barrier, inc=1, device_id={"blk": prv, "rep": 2})

    @pl.when(below)
    def _():
        pl.semaphore_signal(barrier, inc=1, device_id={"blk": nxt, "rep": 3})

    pl.semaphore_wait(barrier, n + m - 2 + jnp.where(jnp.logical_or(above, below), 1, 0))

    keys, started = {}, []

    def copy(name, src, dst, blk, rep):
        key = keys.setdefault(name, len(keys))
        return pltpu.make_async_remote_copy(
            src_ref=src,
            dst_ref=dst,
            send_sem=send_sem.at[key],
            recv_sem=recv_sem.at[key],
            device_id={"blk": blk, "rep": rep},
        )

    def start(made, cond=always):
        started.append((made, cond))
        when(cond, made.start)

    def flush():
        for made, cond in started:
            when(cond, made.wait_send)
        started.clear()

    def half(c):
        return pl.ds(c * cw, cw)

    ahead = lax.rem(p + 2 * r, n)
    after = lax.rem(p + 2 * r + 1, n)
    to_ahead, to_after = moved, odd

    def to_first(c, src, blk, rep):
        return copy(("a", c), src, xs.at[0, c], blk, rep)

    def to_second(c, src, blk, rep):
        return copy(("b", c), src, xs.at[1, c], blk, rep)

    def send_features(c):
        start(to_second(c, feats.at[:, half(c)], after, r), to_after)
        start(to_first(c, feats.at[:, half(c)], ahead, r), to_ahead)

    send_features(0)
    own = [
        pltpu.make_async_copy(feats.at[:, half(c)], xs.at[0, c], load_sem.at[len(pairs) + c])
        for c in range(HALVES)
    ]

    @pl.when(r == 0)
    def _():
        for c in range(HALVES):
            own[c].start()

    for made in loads:
        made.wait()
    for s in range(2):
        if s == 1:
            flush()
            send_features(1)
        owner = lax.rem(p - 2 * r - s + 2 * n, n)
        for b in range(blocks):
            name = owner * blocks + b
            at = slice((s * blocks + b) * size, (s * blocks + b + 1) * size)
            for i in range(blocks):
                tile = jnp.zeros((size, size), F32)
                for k in range(slots):
                    tile = tile + tiles[i, k] * jnp.where(cols[i, k] == name, 1.0, 0.0)
                high, low = split(tile)
                s_hi[i * size : (i + 1) * size, at] = high
                s_lo[i * size : (i + 1) * size, at] = low
                high, low = split(tile.T)
                st_hi[at, i * size : (i + 1) * size] = high
                st_lo[at, i * size : (i + 1) * size] = low

    def take_first(c):
        @pl.when(moved)
        def _():
            to_first(c, xs.at[0, c], p, r).wait_recv()

        @pl.when(r == 0)
        def _():
            own[c].wait()

        start(to_second(c, xs.at[0, c], nxt, r), even)

    def product(c, s):
        at = slice(s * rows, (s + 1) * rows)
        return dot3((s_hi[:, at], s_lo[:, at]), split(xs[s, c]))

    hsends = []

    some = part // ROW_PARTS

    def row_part(s):
        return pl.ds(s * some, some)

    def aggregate_sends(c):
        last_half = c == HALVES - 1
        spans = [row_part(s) for s in range(ROW_PARTS)] if last_half else [pl.ds(0, part)]
        for s, span in enumerate(spans):
            made_s = []
            for d in range(m - 1, 0, -1):
                to = lax.rem(r + d, m)
                made = copy(
                    ("c", c, s, d), hpart.at[c, to, span], hrecv.at[c, d - 1, span], p, to
                )
                start(made)
                made_s.append(made)
            hsends.append(made_s)

    for c in range(HALVES):
        take_first(c)
        acc = product(c, 0)
        to_second(c, xs.at[1, c], p, r).wait_recv()
        acc = acc + product(c, 1)
        hpart[c] = acc.reshape(m, part, cw)
        aggregate_sends(c)
    w = split(weight[...])
    wt = split(weight[...].T)

    def aggregate(c, span):
        received = (hrecv[c, 0, span] + hrecv[c, 1, span]) + hrecv[c, 2, span]
        return hpart[c, r, span] + received

    def times_weight(value, c):
        inner = slice(c * cw, (c + 1) * cw)
        return dot3(split(value), (w[0][inner], w[1][inner]))

    for made in hsends[0]:
        made.wait_recv()
    early = aggregate(0, pl.ds(0, part))
    early_pre = times_weight(early, 0) + bias[...]

    forward = list(started)
    started.clear()

    gsends = [[] for _ in range(HALVES)]
    aggs, gpres = [], []
    for s in range(ROW_PARTS):
        here = slice(s * some, (s + 1) * some)
        for made in hsends[1 + s]:
            made.wait_recv()
        late = aggregate(1, row_part(s))
        pre = early_pre[here] + times_weight(late, 1)
        exped = jnp.exp(jnp.minimum(pre, 0.0))
        gpre = cot[here] * jnp.where(pre > 0, 1.0, exped)
        gpre_parts = split(gpre)
        for c in range(HALVES):
            columns = slice(c * cw, (c + 1) * cw)
            grad[c, r, row_part(s)] = dot3(gpre_parts, (wt[0][:, columns], wt[1][:, columns]))
            if c == 0:
                for d in range(m - 1, 0, -1):
                    to = lax.rem(r + d, m)
                    block = grad.at[c, r, row_part(s)]
                    made = copy(("d", c, s, d), block, block, p, to)
                    start(made)
                    gsends[c].append(made)
        out[here] = jnp.where(pre > 0, pre, exped - 1.0)
        aggs.append(jnp.concatenate([early[here], late], axis=1))
        gpres.append(gpre)
    for d in range(m - 1, 0, -1):
        to = lax.rem(r + d, m)
        made = copy(("d", 1, 0, d), grad.at[1, r], grad.at[1, r], p, to)
        start(made)
        gsends[1].append(made)
    agg = jnp.concatenate(aggs, axis=0)
    gpre = jnp.concatenate(gpres, axis=0)
    gpre_parts = split(gpre)

    gw = dot3(split(agg.T), gpre_parts)
    gb = jnp.broadcast_to(jnp.sum(gpre, axis=0, keepdims=True), (8, width))
    for q in range(n):
        gws[q, :piece] = gw[q * piece : (q + 1) * piece]
        gws[q, piece:] = gb
    gwr[p] = gws[p]
    esends = []
    for d in range(1, n):
        to = lax.rem(p + d, n)
        made = copy(("e", d), gws.at[to], gwr.at[p], to, r)
        start(made)
        esends.append(made)

    def weight_sums():
        for made in esends:
            made.wait_recv()
        total_p = gwr[0]
        for q in range(1, n):
            total_p = total_p + gwr[q]
        gwz[r] = total_p
        made_z = []
        for d in range(m - 1, 0, -1):
            to = lax.rem(r + d, m)
            made = copy(("m", d), gwz.at[r], gwz.at[r], p, to)
            start(made)
            made_z.append(made)
        return made_z

    scale = 1.0 / math.sqrt(rows * n)

    def weight_gather(made_z):
        for made in made_z:
            made.wait_recv()
        whole = gwz[0]
        for q in range(1, m):
            whole = whole + gwz[q]
        gfin[p] = whole[:piece] * scale
        gbias[...] = whole[piece : piece + 1] * scale
        made_n = []
        for d in range(1, n):
            to = lax.rem(p + d, n)
            made = copy(("n", d), gfin.at[p], gfin.at[p], to, r)
            start(made)
            made_n.append(made)
        return made_n

    back = lax.rem(p - 2 * r + n, n)
    before = lax.rem(p - 2 * r - 1 + 2 * n, n)
    order = [m - 1 - j for j in range(m)]

    def place(d):
        return lax.rem(r + d, m)

    def to_fold(c, d, blk):
        b = place(d)
        return copy(("f", c, d), adj.at[1, c, b], fold.at[c, b], blk, r)

    def to_near(c, d):
        b = place(d)
        return copy(("g", c, d), adj.at[0, c, b], extra.at[c, b], nxt, r)

    def to_above(c, b):
        return copy(("h", c, b), adj.at[1, c, b], extra.at[c, b], nxt, r + 1)

    def to_total(c, d):
        b = place(d)
        return copy(("k", c, d), adj.at[0, c, b], total.at[c, b], back, r)

    plain_second = but(but(even, below), near_from)
    plain_first = but(but(both(odd, moved), near_to), above)

    def adjoint(c):
        for made in gsends[c]:
            made.wait_recv()
        g = split(grad[c].reshape(rows, cw))
        adj[1, c] = dot3((st_hi[rows:], st_lo[rows:]), g).reshape(m, part, cw)
        for d in order:
            start(to_fold(c, d, prv), odd)
            start(to_fold(c, d, before), plain_second)
        for b in range(m):
            start(to_above(c, b), below)
        adj[0, c] = dot3((st_hi[:rows], st_lo[:rows]), g).reshape(m, part, cw)
        for d in order:
            start(to_near(c, d), near_to)
            start(to_total(c, d), plain_first)

        @pl.when(even)
        def _():
            for d in order:
                b = place(d)
                to_fold(c, d, prv).wait_recv()
                adj[0, c, b] = adj[0, c, b] + fold[c, b]
                pl.when(moved)(to_total(c, d).start)

        @pl.when(above)
        def _():
            for d in order:
                b = (3 + d) % m
                to_above(c, b).wait_recv()
                adj[0, c, b] = adj[0, c, b] + extra[c, b]
                to_total(c, d).start()

        @pl.when(near_from)
        def _():
            for d in order:
                b = place(d)
                to_near(c, d).wait_recv()
                adj[1, c, b] = adj[1, c, b] + extra[c, b]
                to_fold(c, d, before).start()

        for d in order:
            started.append((to_total(c, d), both(even, moved)))
            started.append((to_total(c, d), above))
            started.append((to_fold(c, d, before), near_from))

    from_total = but(moved, both(r == 1, kind == 3))
    from_fold = but(odd, both(r == 2, kind == 1))

    def adjoint_reduce(c):
        made_c = []
        for d in order:
            b = place(d)

            @pl.when(from_total)
            def _():
                to_total(c, d).wait_recv()

            @pl.when(r == 0)
            def _():
                total[c, b] = adj[0, c, b]

            @pl.when(from_fold)
            def _():
                to_fold(c, d, prv).wait_recv()

                @pl.when(from_total)
                def _():
                    total[c, b] = total[c, b] + fold[c, b]

                @pl.when(r == 0)
                def _():
                    total[c, b] = total[c, b] + fold[c, b]

                @pl.when(both(r == 1, kind == 3))
                def _():
                    total[c, b] = fold[c, b]

            if d:
                made = copy(("l", c, d), total.at[c, b], frecv.at[c, d - 1], p, b)
                start(made)
                made_c.append(made)
        return made_c

    for made, cond in forward:
        when(cond, made.wait_send)
    adjoint(0)
    made_z = weight_sums()
    adjoint(1)
    lsends = [adjoint_reduce(0)]
    made_n = weight_gather(made_z)
    lsends.append(adjoint_reduce(1))
    flush()
    for c in range(HALVES):
        if c == 1:
            for made in made_n:
                made.wait_recv()
            gweight[...] = gfin[...].reshape(width, width)
        for made in lsends[c]:
            made.wait_recv()
        gfeats[:, half(c)] = total[c, r] + ((frecv[c, 0] + frecv[c, 1]) + frecv[c, 2])
    flush()


def store_results(*refs):
    count = len(refs) // 3
    sources, targets, stages = refs[:count], refs[count : 2 * count], refs[2 * count : 3 * count]
    sems = refs[-1]
    loads = [
        pltpu.make_async_copy(sources[i], stages[i], sems.at[0, i]) for i in range(count)
    ]
    stores = [
        pltpu.make_async_copy(stages[i], targets[i], sems.at[1, i]) for i in range(count)
    ]
    for made in loads:
        made.start()
    for load, store in zip(loads, stores):
        load.wait()
        store.start()
    for made in stores:
        made.wait()


def fast_body(n, m, node_feats, operator_tiles, tile_cols, weight, layer_bias, cotangent):
    blocks, _, size, _ = operator_tiles.shape
    rows = blocks * size
    part, width = cotangent.shape
    cw = width // HALVES
    piece = width // n
    copies = HALVES * (2 + 5 * (m - 1) + 4 * m) + 2 * (n - 1) + (m - 1)
    vmem = pl.BlockSpec(memory_space=pltpu.VMEM)
    shape = jax.ShapeDtypeStruct
    quarter = (HALVES, m, part, cw)
    result = pl.pallas_call(
        functools.partial(kernel, n, m),
        out_shape=(
            shape((part, width), F32),
            shape((part, width), F32),
            shape((width, width), F32),
            shape((1, width), F32),
        ),
        in_specs=[pl.BlockSpec(memory_space=pltpu.HBM)] * 6,
        out_specs=(vmem,) * 4,
        scratch_shapes=[
            pltpu.VMEM(operator_tiles.shape, F32),
            pltpu.SMEM(tile_cols.shape, jnp.int32),
            pltpu.VMEM((width, width), F32),
            pltpu.VMEM((1, width), F32),
            pltpu.VMEM((part, width), F32),
            pltpu.VMEM((2, HALVES, rows, cw), F32),
            pltpu.VMEM((rows, 2 * rows), BF16),
            pltpu.VMEM((rows, 2 * rows), BF16),
            pltpu.VMEM((2 * rows, rows), BF16),
            pltpu.VMEM((2 * rows, rows), BF16),
            pltpu.VMEM(quarter, F32),
            pltpu.VMEM((HALVES, m - 1, part, cw), F32),
            pltpu.VMEM(quarter, F32),
            pltpu.VMEM((2,) + quarter, F32),
            pltpu.VMEM(quarter, F32),
            pltpu.VMEM(quarter, F32),
            pltpu.VMEM(quarter, F32),
            pltpu.VMEM((HALVES, m - 1, part, cw), F32),
            pltpu.VMEM((n, piece + 8, width), F32),
            pltpu.VMEM((n, piece + 8, width), F32),
            pltpu.VMEM((m, piece + 8, width), F32),
            pltpu.VMEM((n, piece, width), F32),
            pltpu.SemaphoreType.DMA((copies,)),
            pltpu.SemaphoreType.DMA((copies,)),
            pltpu.SemaphoreType.DMA((5 + HALVES,)),
        ],
        compiler_params=pltpu.CompilerParams(
            collective_id=0, has_side_effects=True, vmem_limit_bytes=63 * 1024 * 1024
        ),
    )(node_feats, operator_tiles, tile_cols, weight, layer_bias.reshape(1, width), cotangent)
    layer_out, grad_feats, grad_weight, grad_bias = pl.pallas_call(
        store_results,
        out_shape=[shape(value.shape, F32) for value in result],
        in_specs=[pl.BlockSpec(memory_space=pl.ANY)] * len(result),
        out_specs=[pl.BlockSpec(memory_space=pl.ANY)] * len(result),
        scratch_shapes=[pltpu.VMEM(value.shape, F32) for value in result]
        + [pltpu.SemaphoreType.DMA((2, len(result)))],
        compiler_params=pltpu.CompilerParams(vmem_limit_bytes=63 * 1024 * 1024),
    )(*result)
    return layer_out, grad_feats, grad_weight, grad_bias.reshape(width)


def solution(mesh):
    n, m = mesh.shape["blk"], mesh.shape["rep"]
    fits = n == 2 * m and m == 4
    return jax.shard_map(
        functools.partial(fast_body, n, m) if fits else body,
        mesh=mesh,
        in_specs=(
            P("blk", None),
            P("blk", "rep", None, None),
            P("blk", "rep"),
            P(),
            P(),
            P(("blk", "rep"), None),
        ),
        out_specs=(P(("blk", "rep"), None), P(("blk", "rep"), None), P(), P()),
        check_vma=False,
    )
```

```python
import functools
import math

import jax
import jax.numpy as jnp
from jax import lax
from jax.experimental import pallas as pl
from jax.experimental.pallas import tpu as pltpu
from jax.sharding import PartitionSpec as P

TOP_PRECISION = lax.Precision.HIGHEST


def shifted_2(value, axis, steps):
    count = lax.axis_size(axis)
    pairs = [(source, (source + steps) % count) for source in range(count)]
    return lax.ppermute(value, axis, pairs)


def body(node_feats, operator_tiles, tile_cols, weight, layer_bias, cotangent):
    cycle_size = lax.axis_size("blk")
    rep_size = lax.axis_size("rep")
    window = cycle_size // rep_size
    position = lax.axis_index("blk")
    replica = lax.axis_index("rep")
    offset = replica * window
    blocks, slot_count, tile_size, _ = operator_tiles.shape
    width = node_feats.shape[1]
    row_count = blocks * tile_size
    owners = tile_cols // blocks
    within = tile_cols % blocks
    distance = jnp.mod(position - owners, cycle_size) - offset
    columns = jnp.arange(blocks, dtype=jnp.int32)
    sections = jnp.arange(window, dtype=jnp.int32)
    chosen = (
        (distance[:, :, None, None] == sections[None, None, :, None])
        & (within[:, :, None, None] == columns[None, None, None, :])
    ).astype(jnp.float32)

    def reshape_to_blocks(rows):
        return rows.reshape(blocks, tile_size, width)

    def store(stacked, section_no, current):
        return lax.dynamic_update_index_in_dim(stacked, reshape_to_blocks(current), section_no, 0)

    aligned = node_feats
    for bit_pos in range(rep_size.bit_length() - 1):
        shifted = shifted_2(aligned, "blk", window << bit_pos)
        aligned = jnp.where((replica >> bit_pos) % 2 == 1, shifted, aligned)
    empty = jnp.zeros((window, blocks, tile_size, width), jnp.float32)

    def advance(section_no, loop_state):
        current, stacked = loop_state
        current = shifted_2(current, "blk", 1)
        return (current, store(stacked, section_no, current))

    _, received = lax.fori_loop(1, window, advance, (aligned, store(empty, 0, aligned)))
    selected_tiles = jnp.einsum("iksc,scbd->ikbd", chosen, received, precision=TOP_PRECISION)
    partial_aggregate = jnp.einsum(
        "uzrj,uzje->ure", operator_tiles, selected_tiles, precision=TOP_PRECISION
    ).reshape(row_count, width)
    aggregated = lax.psum_scatter(partial_aggregate, "rep", scatter_dimension=0, tiled=True)
    pre_act = jnp.dot(aggregated, weight, precision=TOP_PRECISION) + layer_bias
    negative = jnp.minimum(pre_act, 0.0)
    layer_out = jnp.where(pre_act > 0, pre_act, jnp.expm1(negative))
    grad_pre = cotangent * jnp.where(pre_act > 0, 1.0, jnp.exp(negative))
    grad_scale = 1.0 / math.sqrt(row_count * cycle_size)
    grad_weight = (
        jnp.einsum("rd,re->de", aggregated, grad_pre, precision=TOP_PRECISION) * grad_scale
    )
    grad_bias = jnp.sum(grad_pre, axis=0) * grad_scale
    grad_weight, grad_bias = lax.psum((grad_weight, grad_bias), ("blk", "rep"))
    grad_hidden = jnp.einsum("re,de->rd", grad_pre, weight, precision=TOP_PRECISION)
    hidden_gradient = lax.all_gather(grad_hidden, "rep", axis=0, tiled=True)
    slot_terms = jnp.einsum(
        "xszt,xzc->xstc",
        operator_tiles,
        reshape_to_blocks(hidden_gradient),
        precision=TOP_PRECISION,
    )
    sorted_terms = jnp.einsum("iksc,ikbd->scbd", chosen, slot_terms, precision=TOP_PRECISION)

    def adjoint_term(section_no):
        return lax.dynamic_index_in_dim(sorted_terms, section_no, 0, keepdims=False).reshape(
            row_count, width
        )

    def retreat(counter, running):
        moved = shifted_2(running, "blk", -1)
        return moved + adjoint_term(window - 1 - counter)

    adjoint = lax.fori_loop(1, window, retreat, adjoint_term(window - 1))
    for bit_pos in range(rep_size.bit_length() - 1):
        returned = shifted_2(adjoint, "blk", -(window << bit_pos))
        adjoint = jnp.where((replica >> bit_pos) % 2 == 1, returned, adjoint)
    grad_feats = lax.psum_scatter(adjoint, "rep", scatter_dimension=0, tiled=True)
    return (layer_out, grad_feats, grad_weight, grad_bias)


F32, BF16 = jnp.float32, jnp.bfloat16
HALVES = 2
ROW_PARTS = 2


def split(value):
    high = value.astype(BF16)
    return high, (value - high.astype(F32)).astype(BF16)


def dot3(a, b):
    def product(x, y):
        return jnp.dot(x, y, preferred_element_type=F32)

    columns = b[0].shape[1]
    pair = product(a[0], jnp.concatenate([b[0], b[1]], axis=1))
    return pair[:, :columns] + (pair[:, columns:] + product(a[1], b[0]))


def kernel(
    n, m, feats, tiles_hbm, cols_hbm, weight_hbm, bias_hbm, cot_hbm,
    out, gfeats, gweight, gbias,
    tiles, cols, weight, bias, cot,
    xs, s_hi, s_lo, st_hi, st_lo, hpart, hrecv, grad, adj, fold, extra, total, frecv,
    gws, gwr, gwz, gfin, send_sem, recv_sem, load_sem,
):
    p, r = lax.axis_index("blk"), lax.axis_index("rep")
    blocks, slots, size, _ = tiles.shape
    rows = blocks * size
    part, width = cot.shape
    cw = width // HALVES
    piece = width // n
    kind = lax.rem(p, 4)
    even = lax.rem(p, 2) == 0
    odd = jnp.logical_not(even)
    moved = r > 0
    always = None

    def both(x, y):
        return jnp.logical_and(x, y)

    def but(x, y):
        return jnp.logical_and(x, jnp.logical_not(y))

    def when(cond, action):
        if cond is None:
            action()
        else:
            pl.when(cond)(action)

    near_from = both(r == 1, kind == 2)
    near_to = both(r == 1, kind == 1)
    above = both(r == 3, kind == 3)
    below = both(r == 2, kind == 2)
    nxt = lax.rem(p + 1, n)
    prv = lax.rem(p - 1 + n, n)

    pairs = [
        (tiles_hbm, tiles),
        (cols_hbm, cols),
        (weight_hbm, weight),
        (bias_hbm, bias),
        (cot_hbm, cot),
    ]
    loads = [
        pltpu.make_async_copy(src, dst, load_sem.at[i]) for i, (src, dst) in enumerate(pairs)
    ]
    for made in loads:
        made.start()

    barrier = pltpu.get_barrier_semaphore()
    for d in range(1, n):
        pl.semaphore_signal(barrier, inc=1, device_id={"blk": lax.rem(p + d, n), "rep": r})
    for d in range(1, m):
        pl.semaphore_signal(barrier, inc=1, device_id={"blk": p, "rep": lax.rem(r + d, m)})

    @pl.when(above)
    def _():
        pl.semaphore_signal(barrier, inc=1, device_id={"blk": prv, "rep": 2})

    @pl.when(below)
    def _():
        pl.semaphore_signal(barrier, inc=1, device_id={"blk": nxt, "rep": 3})

    pl.semaphore_wait(barrier, n + m - 2 + jnp.where(jnp.logical_or(above, below), 1, 0))

    keys, started = {}, []

    def copy(name, src, dst, blk, rep):
        key = keys.setdefault(name, len(keys))
        return pltpu.make_async_remote_copy(
            src_ref=src,
            dst_ref=dst,
            send_sem=send_sem.at[key],
            recv_sem=recv_sem.at[key],
            device_id={"blk": blk, "rep": rep},
        )

    def start(made, cond=always):
        started.append((made, cond))
        when(cond, made.start)

    def flush():
        for made, cond in started:
            when(cond, made.wait_send)
        started.clear()

    def half(c):
        return pl.ds(c * cw, cw)

    ahead = lax.rem(p + 2 * r, n)
    after = lax.rem(p + 2 * r + 1, n)
    to_ahead, to_after = moved, odd

    def to_first(c, src, blk, rep):
        return copy(("a", c), src, xs.at[0, c], blk, rep)

    def to_second(c, src, blk, rep):
        return copy(("b", c), src, xs.at[1, c], blk, rep)

    def send_features(c):
        start(to_second(c, feats.at[:, half(c)], after, r), to_after)
        start(to_first(c, feats.at[:, half(c)], ahead, r), to_ahead)

    send_features(0)
    own = [
        pltpu.make_async_copy(feats.at[:, half(c)], xs.at[0, c], load_sem.at[len(pairs) + c])
        for c in range(HALVES)
    ]

    @pl.when(r == 0)
    def _():
        for c in range(HALVES):
            own[c].start()

    for made in loads:
        made.wait()
    for s in range(2):
        if s == 1:
            flush()
            send_features(1)
        owner = lax.rem(p - 2 * r - s + 2 * n, n)
        for b in range(blocks):
            name = owner * blocks + b
            at = slice((s * blocks + b) * size, (s * blocks + b + 1) * size)
            for i in range(blocks):
                tile = jnp.zeros((size, size), F32)
                for k in range(slots):
                    tile = tile + tiles[i, k] * jnp.where(cols[i, k] == name, 1.0, 0.0)
                high, low = split(tile)
                s_hi[i * size : (i + 1) * size, at] = high
                s_lo[i * size : (i + 1) * size, at] = low
                high, low = split(tile.T)
                st_hi[at, i * size : (i + 1) * size] = high
                st_lo[at, i * size : (i + 1) * size] = low

    def take_first(c):
        @pl.when(moved)
        def _():
            to_first(c, xs.at[0, c], p, r).wait_recv()

        @pl.when(r == 0)
        def _():
            own[c].wait()

        start(to_second(c, xs.at[0, c], nxt, r), even)

    def product(c, s):
        at = slice(s * rows, (s + 1) * rows)
        return dot3((s_hi[:, at], s_lo[:, at]), split(xs[s, c]))

    hsends = []

    some = part // ROW_PARTS

    def row_part(s):
        return pl.ds(s * some, some)

    def aggregate_sends(c):
        last_half = c == HALVES - 1
        spans = [row_part(s) for s in range(ROW_PARTS)] if last_half else [pl.ds(0, part)]
        for s, span in enumerate(spans):
            made_s = []
            for d in range(m - 1, 0, -1):
                to = lax.rem(r + d, m)
                made = copy(
                    ("c", c, s, d), hpart.at[c, to, span], hrecv.at[c, d - 1, span], p, to
                )
                start(made)
                made_s.append(made)
            hsends.append(made_s)

    for c in range(HALVES):
        take_first(c)
        acc = product(c, 0)
        to_second(c, xs.at[1, c], p, r).wait_recv()
        acc = acc + product(c, 1)
        hpart[c] = acc.reshape(m, part, cw)
        aggregate_sends(c)
    w = split(weight[...])
    wt = split(weight[...].T)

    def aggregate(c, span):
        received = (hrecv[c, 0, span] + hrecv[c, 1, span]) + hrecv[c, 2, span]
        return hpart[c, r, span] + received

    def times_weight(value, c):
        inner = slice(c * cw, (c + 1) * cw)
        return dot3(split(value), (w[0][inner], w[1][inner]))

    for made in hsends[0]:
        made.wait_recv()
    early = aggregate(0, pl.ds(0, part))
    early_pre = times_weight(early, 0) + bias[...]

    forward = list(started)
    started.clear()

    gsends = [[] for _ in range(HALVES)]

    def direct(d):
        if d == m - 1:
            return r != 0
        return r != m - 1 if d == 1 else None

    aggs, gpres = [], []
    for s in range(ROW_PARTS):
        here = slice(s * some, (s + 1) * some)
        for made in hsends[1 + s]:
            made.wait_recv()
        late = aggregate(1, row_part(s))
        pre = early_pre[here] + times_weight(late, 1)
        exped = jnp.exp(jnp.minimum(pre, 0.0))
        gpre = cot[here] * jnp.where(pre > 0, 1.0, exped)
        gpre_parts = split(gpre)
        for c in range(HALVES):
            columns = slice(c * cw, (c + 1) * cw)
            grad[c, r, row_part(s)] = dot3(gpre_parts, (wt[0][:, columns], wt[1][:, columns]))
            if c == 0:
                for d in range(m - 1, 0, -1):
                    to = lax.rem(r + d, m)
                    block = grad.at[c, r, row_part(s)]
                    made = copy(("d", c, s, d), block, block, p, to)
                    start(made, direct(d))
                    gsends[c].append((made, s, d))
        out[here] = jnp.where(pre > 0, pre, exped - 1.0)
        aggs.append(jnp.concatenate([early[here], late], axis=1))
        gpres.append(gpre)
    for d in range(m - 1, 0, -1):
        to = lax.rem(r + d, m)
        made = copy(("d", 1, 0, d), grad.at[1, r], grad.at[1, r], p, to)
        start(made, direct(d))
        gsends[1].append((made, None, d))
    agg = jnp.concatenate(aggs, axis=0)
    gpre = jnp.concatenate(gpres, axis=0)
    gpre_parts = split(gpre)

    gw = dot3(split(agg.T), gpre_parts)
    gb = jnp.broadcast_to(jnp.sum(gpre, axis=0, keepdims=True), (8, width))
    for q in range(n):
        gws[q, :piece] = gw[q * piece : (q + 1) * piece]
        gws[q, piece:] = gb
    gwr[p] = gws[p]
    esends = []
    for d in range(1, n):
        to = lax.rem(p + d, n)
        made = copy(("e", d), gws.at[to], gwr.at[p], to, r)
        start(made)
        esends.append(made)

    def weight_sums():
        for made in esends:
            made.wait_recv()
        total_p = gwr[0]
        for q in range(1, n):
            total_p = total_p + gwr[q]
        gwz[r] = total_p
        made_z = []
        for d in range(m - 1, 0, -1):
            to = lax.rem(r + d, m)
            made = copy(("m", d), gwz.at[r], gwz.at[r], p, to)
            start(made)
            made_z.append(made)
        return made_z

    scale = 1.0 / math.sqrt(rows * n)

    def weight_gather(made_z):
        for made in made_z:
            made.wait_recv()
        whole = gwz[0]
        for q in range(1, m):
            whole = whole + gwz[q]
        gfin[p] = whole[:piece] * scale
        gbias[...] = whole[piece : piece + 1] * scale
        made_n = []
        for d in range(1, n):
            to = lax.rem(p + d, n)
            made = copy(("n", d), gfin.at[p], gfin.at[p], to, r)
            start(made)
            made_n.append(made)
        return made_n

    back = lax.rem(p - 2 * r + n, n)
    before = lax.rem(p - 2 * r - 1 + 2 * n, n)
    order = [m - 1 - j for j in range(m)]

    def place(d):
        return lax.rem(r + d, m)

    def to_fold(c, d, blk):
        b = place(d)
        return copy(("f", c, d), adj.at[1, c, b], fold.at[c, b], blk, r)

    def to_near(c, d):
        b = place(d)
        return copy(("g", c, d), adj.at[0, c, b], extra.at[c, b], nxt, r)

    def to_above(c, b):
        return copy(("h", c, b), adj.at[1, c, b], extra.at[c, b], nxt, r + 1)

    def to_total(c, d):
        b = place(d)
        return copy(("k", c, d), adj.at[0, c, b], total.at[c, b], back, r)

    plain_second = but(but(even, below), near_from)
    plain_first = but(but(both(odd, moved), near_to), above)

    def adjoint(c):
        for made, s, d in gsends[c]:
            if d != 2:
                continue
            made.wait_recv()
            for source, via, to, key in ((0, 2, 3, 3), (3, 1, 0, 1)):
                block = grad.at[c, source] if s is None else grad.at[c, source, row_part(s)]
                passed = copy(("d", c, s or 0, key), block, block, p, to)
                start(passed, r == via)
        for made, s, d in gsends[c]:
            if d != 2:
                made.wait_recv()
        g = split(grad[c].reshape(rows, cw))
        adj[1, c] = dot3((st_hi[rows:], st_lo[rows:]), g).reshape(m, part, cw)
        for d in order:
            start(to_fold(c, d, prv), odd)
            start(to_fold(c, d, before), plain_second)
        for b in range(m):
            start(to_above(c, b), below)
        adj[0, c] = dot3((st_hi[:rows], st_lo[:rows]), g).reshape(m, part, cw)
        for d in order:
            start(to_near(c, d), near_to)
            start(to_total(c, d), plain_first)

        @pl.when(even)
        def _():
            for d in order:
                b = place(d)
                to_fold(c, d, prv).wait_recv()
                adj[0, c, b] = adj[0, c, b] + fold[c, b]
                pl.when(moved)(to_total(c, d).start)

        @pl.when(above)
        def _():
            for d in order:
                b = (3 + d) % m
                to_above(c, b).wait_recv()
                adj[0, c, b] = adj[0, c, b] + extra[c, b]
                to_total(c, d).start()

        @pl.when(near_from)
        def _():
            for d in order:
                b = place(d)
                to_near(c, d).wait_recv()
                adj[1, c, b] = adj[1, c, b] + extra[c, b]
                to_fold(c, d, before).start()

        for d in order:
            started.append((to_total(c, d), both(even, moved)))
            started.append((to_total(c, d), above))
            started.append((to_fold(c, d, before), near_from))

    from_total = but(moved, both(r == 1, kind == 3))
    from_fold = but(odd, both(r == 2, kind == 1))

    def adjoint_reduce(c):
        made_c = []
        for d in order:
            b = place(d)

            @pl.when(from_total)
            def _():
                to_total(c, d).wait_recv()

            @pl.when(r == 0)
            def _():
                total[c, b] = adj[0, c, b]

            @pl.when(from_fold)
            def _():
                to_fold(c, d, prv).wait_recv()

                @pl.when(from_total)
                def _():
                    total[c, b] = total[c, b] + fold[c, b]

                @pl.when(r == 0)
                def _():
                    total[c, b] = total[c, b] + fold[c, b]

                @pl.when(both(r == 1, kind == 3))
                def _():
                    total[c, b] = fold[c, b]

            if d:
                made = copy(("l", c, d), total.at[c, b], frecv.at[c, d - 1], p, b)
                start(made)
                made_c.append(made)
        return made_c

    for made, cond in forward:
        when(cond, made.wait_send)
    adjoint(0)
    made_z = weight_sums()
    adjoint(1)
    lsends = [adjoint_reduce(0)]
    made_n = weight_gather(made_z)
    lsends.append(adjoint_reduce(1))
    flush()
    for c in range(HALVES):
        if c == 1:
            for made in made_n:
                made.wait_recv()
            gweight[...] = gfin[...].reshape(width, width)
        for made in lsends[c]:
            made.wait_recv()
        gfeats[:, half(c)] = total[c, r] + ((frecv[c, 0] + frecv[c, 1]) + frecv[c, 2])
    flush()


def store_results(*refs):
    count = len(refs) // 3
    sources, targets, stages = refs[:count], refs[count : 2 * count], refs[2 * count : 3 * count]
    sems = refs[-1]
    loads = [
        pltpu.make_async_copy(sources[i], stages[i], sems.at[0, i]) for i in range(count)
    ]
    stores = [
        pltpu.make_async_copy(stages[i], targets[i], sems.at[1, i]) for i in range(count)
    ]
    for made in loads:
        made.start()
    for load, store in zip(loads, stores):
        load.wait()
        store.start()
    for made in stores:
        made.wait()


def fast_body(n, m, node_feats, operator_tiles, tile_cols, weight, layer_bias, cotangent):
    blocks, _, size, _ = operator_tiles.shape
    rows = blocks * size
    part, width = cotangent.shape
    cw = width // HALVES
    piece = width // n
    copies = HALVES * (2 + 5 * (m - 1) + 4 * m) + 2 * (n - 1) + (m - 1)
    vmem = pl.BlockSpec(memory_space=pltpu.VMEM)
    shape = jax.ShapeDtypeStruct
    quarter = (HALVES, m, part, cw)
    result = pl.pallas_call(
        functools.partial(kernel, n, m),
        out_shape=(
            shape((part, width), F32),
            shape((part, width), F32),
            shape((width, width), F32),
            shape((1, width), F32),
        ),
        in_specs=[pl.BlockSpec(memory_space=pltpu.HBM)] * 6,
        out_specs=(vmem,) * 4,
        scratch_shapes=[
            pltpu.VMEM(operator_tiles.shape, F32),
            pltpu.SMEM(tile_cols.shape, jnp.int32),
            pltpu.VMEM((width, width), F32),
            pltpu.VMEM((1, width), F32),
            pltpu.VMEM((part, width), F32),
            pltpu.VMEM((2, HALVES, rows, cw), F32),
            pltpu.VMEM((rows, 2 * rows), BF16),
            pltpu.VMEM((rows, 2 * rows), BF16),
            pltpu.VMEM((2 * rows, rows), BF16),
            pltpu.VMEM((2 * rows, rows), BF16),
            pltpu.VMEM(quarter, F32),
            pltpu.VMEM((HALVES, m - 1, part, cw), F32),
            pltpu.VMEM(quarter, F32),
            pltpu.VMEM((2,) + quarter, F32),
            pltpu.VMEM(quarter, F32),
            pltpu.VMEM(quarter, F32),
            pltpu.VMEM(quarter, F32),
            pltpu.VMEM((HALVES, m - 1, part, cw), F32),
            pltpu.VMEM((n, piece + 8, width), F32),
            pltpu.VMEM((n, piece + 8, width), F32),
            pltpu.VMEM((m, piece + 8, width), F32),
            pltpu.VMEM((n, piece, width), F32),
            pltpu.SemaphoreType.DMA((copies,)),
            pltpu.SemaphoreType.DMA((copies,)),
            pltpu.SemaphoreType.DMA((5 + HALVES,)),
        ],
        compiler_params=pltpu.CompilerParams(
            collective_id=0, has_side_effects=True, vmem_limit_bytes=63 * 1024 * 1024
        ),
    )(node_feats, operator_tiles, tile_cols, weight, layer_bias.reshape(1, width), cotangent)
    layer_out, grad_feats, grad_weight, grad_bias = pl.pallas_call(
        store_results,
        out_shape=[shape(value.shape, F32) for value in result],
        in_specs=[pl.BlockSpec(memory_space=pl.ANY)] * len(result),
        out_specs=[pl.BlockSpec(memory_space=pl.ANY)] * len(result),
        scratch_shapes=[pltpu.VMEM(value.shape, F32) for value in result]
        + [pltpu.SemaphoreType.DMA((2, len(result)))],
        compiler_params=pltpu.CompilerParams(vmem_limit_bytes=63 * 1024 * 1024),
    )(*result)
    return layer_out, grad_feats, grad_weight, grad_bias.reshape(width)


def solution(mesh):
    n, m = mesh.shape["blk"], mesh.shape["rep"]
    fits = n == 2 * m and m == 4
    return jax.shard_map(
        functools.partial(fast_body, n, m) if fits else body,
        mesh=mesh,
        in_specs=(
            P("blk", None),
            P("blk", "rep", None, None),
            P("blk", "rep"),
            P(),
            P(),
            P(("blk", "rep"), None),
        ),
        out_specs=(P(("blk", "rep"), None), P(("blk", "rep"), None), P(), P()),
        check_vma=False,
    )
```

```python
import functools
import math

import jax
import jax.numpy as jnp
from jax import lax
from jax.experimental import pallas as pl
from jax.experimental.pallas import tpu as pltpu
from jax.sharding import PartitionSpec as P

TOP_PRECISION = lax.Precision.HIGHEST


def shifted_2(value, axis, steps):
    count = lax.axis_size(axis)
    pairs = [(source, (source + steps) % count) for source in range(count)]
    return lax.ppermute(value, axis, pairs)


def body(node_feats, operator_tiles, tile_cols, weight, layer_bias, cotangent):
    cycle_size = lax.axis_size("blk")
    rep_size = lax.axis_size("rep")
    window = cycle_size // rep_size
    position = lax.axis_index("blk")
    replica = lax.axis_index("rep")
    offset = replica * window
    blocks, slot_count, tile_size, _ = operator_tiles.shape
    width = node_feats.shape[1]
    row_count = blocks * tile_size
    owners = tile_cols // blocks
    within = tile_cols % blocks
    distance = jnp.mod(position - owners, cycle_size) - offset
    columns = jnp.arange(blocks, dtype=jnp.int32)
    sections = jnp.arange(window, dtype=jnp.int32)
    chosen = (
        (distance[:, :, None, None] == sections[None, None, :, None])
        & (within[:, :, None, None] == columns[None, None, None, :])
    ).astype(jnp.float32)

    def reshape_to_blocks(rows):
        return rows.reshape(blocks, tile_size, width)

    def store(stacked, section_no, current):
        return lax.dynamic_update_index_in_dim(stacked, reshape_to_blocks(current), section_no, 0)

    aligned = node_feats
    for bit_pos in range(rep_size.bit_length() - 1):
        shifted = shifted_2(aligned, "blk", window << bit_pos)
        aligned = jnp.where((replica >> bit_pos) % 2 == 1, shifted, aligned)
    empty = jnp.zeros((window, blocks, tile_size, width), jnp.float32)

    def advance(section_no, loop_state):
        current, stacked = loop_state
        current = shifted_2(current, "blk", 1)
        return (current, store(stacked, section_no, current))

    _, received = lax.fori_loop(1, window, advance, (aligned, store(empty, 0, aligned)))
    selected_tiles = jnp.einsum("iksc,scbd->ikbd", chosen, received, precision=TOP_PRECISION)
    partial_aggregate = jnp.einsum(
        "uzrj,uzje->ure", operator_tiles, selected_tiles, precision=TOP_PRECISION
    ).reshape(row_count, width)
    aggregated = lax.psum_scatter(partial_aggregate, "rep", scatter_dimension=0, tiled=True)
    pre_act = jnp.dot(aggregated, weight, precision=TOP_PRECISION) + layer_bias
    negative = jnp.minimum(pre_act, 0.0)
    layer_out = jnp.where(pre_act > 0, pre_act, jnp.expm1(negative))
    grad_pre = cotangent * jnp.where(pre_act > 0, 1.0, jnp.exp(negative))
    grad_scale = 1.0 / math.sqrt(row_count * cycle_size)
    grad_weight = (
        jnp.einsum("rd,re->de", aggregated, grad_pre, precision=TOP_PRECISION) * grad_scale
    )
    grad_bias = jnp.sum(grad_pre, axis=0) * grad_scale
    grad_weight, grad_bias = lax.psum((grad_weight, grad_bias), ("blk", "rep"))
    grad_hidden = jnp.einsum("re,de->rd", grad_pre, weight, precision=TOP_PRECISION)
    hidden_gradient = lax.all_gather(grad_hidden, "rep", axis=0, tiled=True)
    slot_terms = jnp.einsum(
        "xszt,xzc->xstc",
        operator_tiles,
        reshape_to_blocks(hidden_gradient),
        precision=TOP_PRECISION,
    )
    sorted_terms = jnp.einsum("iksc,ikbd->scbd", chosen, slot_terms, precision=TOP_PRECISION)

    def adjoint_term(section_no):
        return lax.dynamic_index_in_dim(sorted_terms, section_no, 0, keepdims=False).reshape(
            row_count, width
        )

    def retreat(counter, running):
        moved = shifted_2(running, "blk", -1)
        return moved + adjoint_term(window - 1 - counter)

    adjoint = lax.fori_loop(1, window, retreat, adjoint_term(window - 1))
    for bit_pos in range(rep_size.bit_length() - 1):
        returned = shifted_2(adjoint, "blk", -(window << bit_pos))
        adjoint = jnp.where((replica >> bit_pos) % 2 == 1, returned, adjoint)
    grad_feats = lax.psum_scatter(adjoint, "rep", scatter_dimension=0, tiled=True)
    return (layer_out, grad_feats, grad_weight, grad_bias)


F32, BF16 = jnp.float32, jnp.bfloat16
HALVES = 2
ROW_PARTS = 2


def split(value):
    high = value.astype(BF16)
    return high, (value - high.astype(F32)).astype(BF16)


def dot3(a, b):
    def product(x, y):
        return jnp.dot(x, y, preferred_element_type=F32)

    columns = b[0].shape[1]
    pair = product(a[0], jnp.concatenate([b[0], b[1]], axis=1))
    return pair[:, :columns] + (pair[:, columns:] + product(a[1], b[0]))


def kernel(
    n, m, feats, tiles_hbm, cols_hbm, weight_hbm, bias_hbm, cot_hbm,
    out, gfeats, gweight, gbias,
    tiles, cols, weight, bias, cot,
    xs, s_hi, s_lo, st_hi, st_lo, hpart, hrecv, grad, adj, fold, total, frecv,
    gws, gwr, gwz, gfin, send_sem, recv_sem, load_sem,
):
    p, r = lax.axis_index("blk"), lax.axis_index("rep")
    blocks, slots, size, _ = tiles.shape
    rows = blocks * size
    part, width = cot.shape
    cw = width // HALVES
    piece = width // n
    even = lax.rem(p, 2) == 0
    odd = jnp.logical_not(even)
    moved = r > 0
    always = None

    def both(x, y):
        return jnp.logical_and(x, y)

    def when(cond, action):
        if cond is None:
            action()
        else:
            pl.when(cond)(action)

    nxt = lax.rem(p + 1, n)
    prv = lax.rem(p - 1 + n, n)

    pairs = [
        (tiles_hbm, tiles),
        (cols_hbm, cols),
        (weight_hbm, weight),
        (bias_hbm, bias),
        (cot_hbm, cot),
    ]
    loads = [
        pltpu.make_async_copy(src, dst, load_sem.at[i]) for i, (src, dst) in enumerate(pairs)
    ]
    for made in loads:
        made.start()

    barrier = pltpu.get_barrier_semaphore()
    for d in range(1, n):
        pl.semaphore_signal(barrier, inc=1, device_id={"blk": lax.rem(p + d, n), "rep": r})
    for d in range(1, m):
        pl.semaphore_signal(barrier, inc=1, device_id={"blk": p, "rep": lax.rem(r + d, m)})

    pl.semaphore_wait(barrier, n + m - 2)

    keys, started = {}, []

    def copy(name, src, dst, blk, rep):
        key = keys.setdefault(name, len(keys))
        return pltpu.make_async_remote_copy(
            src_ref=src,
            dst_ref=dst,
            send_sem=send_sem.at[key],
            recv_sem=recv_sem.at[key],
            device_id={"blk": blk, "rep": rep},
        )

    def start(made, cond=always):
        started.append((made, cond))
        when(cond, made.start)

    def flush():
        for made, cond in started:
            when(cond, made.wait_send)
        started.clear()

    def half(c):
        return pl.ds(c * cw, cw)

    ahead = lax.rem(p + 2 * r, n)
    after = lax.rem(p + 2 * r + 1, n)
    to_ahead, to_after = moved, odd

    def to_first(c, src, blk, rep):
        return copy(("a", c), src, xs.at[0, c], blk, rep)

    def to_second(c, src, blk, rep):
        return copy(("b", c), src, xs.at[1, c], blk, rep)

    def send_features(c):
        start(to_second(c, feats.at[:, half(c)], after, r), to_after)
        start(to_first(c, feats.at[:, half(c)], ahead, r), to_ahead)

    send_features(0)
    own = [
        pltpu.make_async_copy(feats.at[:, half(c)], xs.at[0, c], load_sem.at[len(pairs) + c])
        for c in range(HALVES)
    ]

    @pl.when(r == 0)
    def _():
        for c in range(HALVES):
            own[c].start()

    for made in loads:
        made.wait()
    for s in range(2):
        owner = lax.rem(p - 2 * r - s + 2 * n, n)
        for b in range(blocks):
            name = owner * blocks + b
            at = slice((s * blocks + b) * size, (s * blocks + b + 1) * size)
            for i in range(blocks):
                tile = jnp.zeros((size, size), F32)
                for k in range(slots):
                    tile = tile + tiles[i, k] * jnp.where(cols[i, k] == name, 1.0, 0.0)
                high, low = split(tile)
                s_hi[i * size : (i + 1) * size, at] = high
                s_lo[i * size : (i + 1) * size, at] = low
                high, low = split(tile.T)
                st_hi[at, i * size : (i + 1) * size] = high
                st_lo[at, i * size : (i + 1) * size] = low

    flush()
    send_features(1)

    def take_first(c):
        @pl.when(moved)
        def _():
            to_first(c, xs.at[0, c], p, r).wait_recv()

        @pl.when(r == 0)
        def _():
            own[c].wait()

        start(to_second(c, xs.at[0, c], nxt, r), even)

    def product(c, s):
        at = slice(s * rows, (s + 1) * rows)
        return dot3((s_hi[:, at], s_lo[:, at]), split(xs[s, c]))

    hsends = []

    some = part // ROW_PARTS

    def row_part(s):
        return pl.ds(s * some, some)

    def aggregate_sends(c):
        last_half = c == HALVES - 1
        spans = [row_part(s) for s in range(ROW_PARTS)] if last_half else [pl.ds(0, part)]
        for s, span in enumerate(spans):
            made_s = []
            for d in range(m - 1, 0, -1):
                to = lax.rem(r + d, m)
                made = copy(
                    ("c", c, s, d), hpart.at[c, to, span], hrecv.at[c, d - 1, span], p, to
                )
                start(made)
                made_s.append(made)
            hsends.append(made_s)

    for c in range(HALVES):
        take_first(c)
        acc = product(c, 0)
        to_second(c, xs.at[1, c], p, r).wait_recv()
        acc = acc + product(c, 1)
        hpart[c] = acc.reshape(m, part, cw)
        aggregate_sends(c)
    w = split(weight[...])
    wt = split(weight[...].T)

    def aggregate(c, span):
        received = (hrecv[c, 0, span] + hrecv[c, 1, span]) + hrecv[c, 2, span]
        return hpart[c, r, span] + received

    def times_weight(value, c):
        inner = slice(c * cw, (c + 1) * cw)
        return dot3(split(value), (w[0][inner], w[1][inner]))

    for made in hsends[0]:
        made.wait_recv()
    early = aggregate(0, pl.ds(0, part))
    early_pre = times_weight(early, 0) + bias[...]

    forward = list(started)
    started.clear()

    gsends = [[] for _ in range(HALVES)]

    def direct(d):
        if d == m - 1:
            return r != 0
        return r != m - 1 if d == 1 else None

    aggs, gpres = [], []
    for s in range(ROW_PARTS):
        here = slice(s * some, (s + 1) * some)
        for made in hsends[1 + s]:
            made.wait_recv()
        late = aggregate(1, row_part(s))
        pre = early_pre[here] + times_weight(late, 1)
        exped = jnp.exp(jnp.minimum(pre, 0.0))
        gpre = cot[here] * jnp.where(pre > 0, 1.0, exped)
        gpre_parts = split(gpre)
        for c in range(HALVES):
            columns = slice(c * cw, (c + 1) * cw)
            grad[c, r, row_part(s)] = dot3(gpre_parts, (wt[0][:, columns], wt[1][:, columns]))
            if c == 0:
                for d in range(m - 1, 0, -1):
                    to = lax.rem(r + d, m)
                    block = grad.at[c, r, row_part(s)]
                    made = copy(("d", c, s, d), block, block, p, to)
                    start(made, direct(d))
                    gsends[c].append((made, s, d))
        out[here] = jnp.where(pre > 0, pre, exped - 1.0)
        aggs.append(jnp.concatenate([early[here], late], axis=1))
        gpres.append(gpre)
    for d in range(m - 1, 0, -1):
        to = lax.rem(r + d, m)
        made = copy(("d", 1, 0, d), grad.at[1, r], grad.at[1, r], p, to)
        start(made, direct(d))
        gsends[1].append((made, None, d))
    agg = jnp.concatenate(aggs, axis=0)
    gpre = jnp.concatenate(gpres, axis=0)
    gpre_parts = split(gpre)

    gw = dot3(split(agg.T), gpre_parts)
    gb = jnp.broadcast_to(jnp.sum(gpre, axis=0, keepdims=True), (8, width))
    for q in range(n):
        gws[q, :piece] = gw[q * piece : (q + 1) * piece]
        gws[q, piece:] = gb
    gwr[p] = gws[p]
    esends = []
    for d in range(1, n):
        to = lax.rem(p + d, n)
        made = copy(("e", d), gws.at[to], gwr.at[p], to, r)
        start(made)
        esends.append(made)

    def weight_sums():
        for made in esends:
            made.wait_recv()
        total_p = gwr[0]
        for q in range(1, n):
            total_p = total_p + gwr[q]
        gwz[r] = total_p
        made_z = []
        for d in range(m - 1, 0, -1):
            to = lax.rem(r + d, m)
            made = copy(("m", d), gwz.at[r], gwz.at[r], p, to)
            start(made)
            made_z.append(made)
        return made_z

    scale = 1.0 / math.sqrt(rows * n)

    def weight_gather(made_z):
        for made in made_z:
            made.wait_recv()
        whole = gwz[0]
        for q in range(1, m):
            whole = whole + gwz[q]
        gfin[p] = whole[:piece] * scale
        gbias[...] = whole[piece : piece + 1] * scale
        made_n = []
        for d in range(1, n):
            to = lax.rem(p + d, n)
            made = copy(("n", d), gfin.at[p], gfin.at[p], to, r)
            start(made)
            made_n.append(made)
        return made_n

    back = lax.rem(p - 2 * r + n, n)
    before = lax.rem(p - 2 * r - 1 + 2 * n, n)
    order = [m - 1 - j for j in range(m)]

    def place(d):
        return lax.rem(r + d, m)

    def to_fold(c, d, blk):
        b = place(d)
        return copy(("f", c, d), adj.at[1, c, b], fold.at[c, b], blk, r)

    def to_total(c, d):
        b = place(d)
        return copy(("k", c, d), adj.at[0, c, b], total.at[c, b], back, r)

    def adjoint(c):
        for made, s, d in gsends[c]:
            if d != 2:
                continue
            made.wait_recv()
            for source, via, to, key in ((0, 2, 3, 3), (3, 1, 0, 1)):
                block = grad.at[c, source] if s is None else grad.at[c, source, row_part(s)]
                passed = copy(("d", c, s or 0, key), block, block, p, to)
                start(passed, r == via)
        for made, s, d in gsends[c]:
            if d != 2:
                made.wait_recv()
        g = split(grad[c].reshape(rows, cw))
        adj[1, c] = dot3((st_hi[rows:], st_lo[rows:]), g).reshape(m, part, cw)
        for d in order:
            start(to_fold(c, d, prv), odd)
            start(to_fold(c, d, before), even)
        adj[0, c] = dot3((st_hi[:rows], st_lo[:rows]), g).reshape(m, part, cw)
        for d in order:
            start(to_total(c, d), both(odd, moved))

        @pl.when(even)
        def _():
            for d in order:
                b = place(d)
                to_fold(c, d, prv).wait_recv()
                adj[0, c, b] = adj[0, c, b] + fold[c, b]
                pl.when(moved)(to_total(c, d).start)

        for d in order:
            started.append((to_total(c, d), both(even, moved)))


    def adjoint_reduce(c):
        made_c = []
        for d in order:
            b = place(d)

            @pl.when(moved)
            def _():
                to_total(c, d).wait_recv()

            @pl.when(r == 0)
            def _():
                total[c, b] = adj[0, c, b]

            @pl.when(odd)
            def _():
                to_fold(c, d, prv).wait_recv()
                total[c, b] = total[c, b] + fold[c, b]

            if d:
                made = copy(("l", c, d), total.at[c, b], frecv.at[c, d - 1], p, b)
                start(made)
                made_c.append(made)
        return made_c

    for made, cond in forward:
        when(cond, made.wait_send)
    adjoint(0)
    made_z = weight_sums()
    adjoint(1)
    lsends = [adjoint_reduce(0)]
    made_n = weight_gather(made_z)
    lsends.append(adjoint_reduce(1))
    flush()
    for c in range(HALVES):
        if c == 1:
            for made in made_n:
                made.wait_recv()
            gweight[...] = gfin[...].reshape(width, width)
        for made in lsends[c]:
            made.wait_recv()
        gfeats[:, half(c)] = total[c, r] + ((frecv[c, 0] + frecv[c, 1]) + frecv[c, 2])
    flush()


def store_results(*refs):
    count = len(refs) // 3
    sources, targets, stages = refs[:count], refs[count : 2 * count], refs[2 * count : 3 * count]
    sems = refs[-1]
    loads = [
        pltpu.make_async_copy(sources[i], stages[i], sems.at[0, i]) for i in range(count)
    ]
    stores = [
        pltpu.make_async_copy(stages[i], targets[i], sems.at[1, i]) for i in range(count)
    ]
    for made in loads:
        made.start()
    for load, store in zip(loads, stores):
        load.wait()
        store.start()
    for made in stores:
        made.wait()


def fast_body(n, m, node_feats, operator_tiles, tile_cols, weight, layer_bias, cotangent):
    blocks, _, size, _ = operator_tiles.shape
    rows = blocks * size
    part, width = cotangent.shape
    cw = width // HALVES
    piece = width // n
    copies = HALVES * (2 + 5 * (m - 1) + 4 * m) + 2 * (n - 1) + (m - 1)
    vmem = pl.BlockSpec(memory_space=pltpu.VMEM)
    shape = jax.ShapeDtypeStruct
    quarter = (HALVES, m, part, cw)
    result = pl.pallas_call(
        functools.partial(kernel, n, m),
        out_shape=(
            shape((part, width), F32),
            shape((part, width), F32),
            shape((width, width), F32),
            shape((1, width), F32),
        ),
        in_specs=[pl.BlockSpec(memory_space=pltpu.HBM)] * 6,
        out_specs=(vmem,) * 4,
        scratch_shapes=[
            pltpu.VMEM(operator_tiles.shape, F32),
            pltpu.SMEM(tile_cols.shape, jnp.int32),
            pltpu.VMEM((width, width), F32),
            pltpu.VMEM((1, width), F32),
            pltpu.VMEM((part, width), F32),
            pltpu.VMEM((2, HALVES, rows, cw), F32),
            pltpu.VMEM((rows, 2 * rows), BF16),
            pltpu.VMEM((rows, 2 * rows), BF16),
            pltpu.VMEM((2 * rows, rows), BF16),
            pltpu.VMEM((2 * rows, rows), BF16),
            pltpu.VMEM(quarter, F32),
            pltpu.VMEM((HALVES, m - 1, part, cw), F32),
            pltpu.VMEM(quarter, F32),
            pltpu.VMEM((2,) + quarter, F32),
            pltpu.VMEM(quarter, F32),
            pltpu.VMEM(quarter, F32),
            pltpu.VMEM((HALVES, m - 1, part, cw), F32),
            pltpu.VMEM((n, piece + 8, width), F32),
            pltpu.VMEM((n, piece + 8, width), F32),
            pltpu.VMEM((m, piece + 8, width), F32),
            pltpu.VMEM((n, piece, width), F32),
            pltpu.SemaphoreType.DMA((copies,)),
            pltpu.SemaphoreType.DMA((copies,)),
            pltpu.SemaphoreType.DMA((5 + HALVES,)),
        ],
        compiler_params=pltpu.CompilerParams(
            collective_id=0, has_side_effects=True, vmem_limit_bytes=63 * 1024 * 1024
        ),
    )(node_feats, operator_tiles, tile_cols, weight, layer_bias.reshape(1, width), cotangent)
    layer_out, grad_feats, grad_weight, grad_bias = pl.pallas_call(
        store_results,
        out_shape=[shape(value.shape, F32) for value in result],
        in_specs=[pl.BlockSpec(memory_space=pl.ANY)] * len(result),
        out_specs=[pl.BlockSpec(memory_space=pl.ANY)] * len(result),
        scratch_shapes=[pltpu.VMEM(value.shape, F32) for value in result]
        + [pltpu.SemaphoreType.DMA((2, len(result)))],
        compiler_params=pltpu.CompilerParams(vmem_limit_bytes=63 * 1024 * 1024),
    )(*result)
    return layer_out, grad_feats, grad_weight, grad_bias.reshape(width)


def solution(mesh):
    n, m = mesh.shape["blk"], mesh.shape["rep"]
    fits = n == 2 * m and m == 4
    return jax.shard_map(
        functools.partial(fast_body, n, m) if fits else body,
        mesh=mesh,
        in_specs=(
            P("blk", None),
            P("blk", "rep", None, None),
            P("blk", "rep"),
            P(),
            P(),
            P(("blk", "rep"), None),
        ),
        out_specs=(P(("blk", "rep"), None), P(("blk", "rep"), None), P(), P()),
        check_vma=False,
    )
```

```python
import functools
import math

import jax
import jax.numpy as jnp
from jax import lax
from jax.experimental import pallas as pl
from jax.experimental.pallas import tpu as pltpu
from jax.sharding import PartitionSpec as P

TOP_PRECISION = lax.Precision.HIGHEST


def shifted_2(value, axis, steps):
    count = lax.axis_size(axis)
    pairs = [(source, (source + steps) % count) for source in range(count)]
    return lax.ppermute(value, axis, pairs)


def body(node_feats, operator_tiles, tile_cols, weight, layer_bias, cotangent):
    cycle_size = lax.axis_size("blk")
    rep_size = lax.axis_size("rep")
    window = cycle_size // rep_size
    position = lax.axis_index("blk")
    replica = lax.axis_index("rep")
    offset = replica * window
    blocks, slot_count, tile_size, _ = operator_tiles.shape
    width = node_feats.shape[1]
    row_count = blocks * tile_size
    owners = tile_cols // blocks
    within = tile_cols % blocks
    distance = jnp.mod(position - owners, cycle_size) - offset
    columns = jnp.arange(blocks, dtype=jnp.int32)
    sections = jnp.arange(window, dtype=jnp.int32)
    chosen = (
        (distance[:, :, None, None] == sections[None, None, :, None])
        & (within[:, :, None, None] == columns[None, None, None, :])
    ).astype(jnp.float32)

    def reshape_to_blocks(rows):
        return rows.reshape(blocks, tile_size, width)

    def store(stacked, section_no, current):
        return lax.dynamic_update_index_in_dim(stacked, reshape_to_blocks(current), section_no, 0)

    aligned = node_feats
    for bit_pos in range(rep_size.bit_length() - 1):
        shifted = shifted_2(aligned, "blk", window << bit_pos)
        aligned = jnp.where((replica >> bit_pos) % 2 == 1, shifted, aligned)
    empty = jnp.zeros((window, blocks, tile_size, width), jnp.float32)

    def advance(section_no, loop_state):
        current, stacked = loop_state
        current = shifted_2(current, "blk", 1)
        return (current, store(stacked, section_no, current))

    _, received = lax.fori_loop(1, window, advance, (aligned, store(empty, 0, aligned)))
    selected_tiles = jnp.einsum("iksc,scbd->ikbd", chosen, received, precision=TOP_PRECISION)
    partial_aggregate = jnp.einsum(
        "uzrj,uzje->ure", operator_tiles, selected_tiles, precision=TOP_PRECISION
    ).reshape(row_count, width)
    aggregated = lax.psum_scatter(partial_aggregate, "rep", scatter_dimension=0, tiled=True)
    pre_act = jnp.dot(aggregated, weight, precision=TOP_PRECISION) + layer_bias
    negative = jnp.minimum(pre_act, 0.0)
    layer_out = jnp.where(pre_act > 0, pre_act, jnp.expm1(negative))
    grad_pre = cotangent * jnp.where(pre_act > 0, 1.0, jnp.exp(negative))
    grad_scale = 1.0 / math.sqrt(row_count * cycle_size)
    grad_weight = (
        jnp.einsum("rd,re->de", aggregated, grad_pre, precision=TOP_PRECISION) * grad_scale
    )
    grad_bias = jnp.sum(grad_pre, axis=0) * grad_scale
    grad_weight, grad_bias = lax.psum((grad_weight, grad_bias), ("blk", "rep"))
    grad_hidden = jnp.einsum("re,de->rd", grad_pre, weight, precision=TOP_PRECISION)
    hidden_gradient = lax.all_gather(grad_hidden, "rep", axis=0, tiled=True)
    slot_terms = jnp.einsum(
        "xszt,xzc->xstc",
        operator_tiles,
        reshape_to_blocks(hidden_gradient),
        precision=TOP_PRECISION,
    )
    sorted_terms = jnp.einsum("iksc,ikbd->scbd", chosen, slot_terms, precision=TOP_PRECISION)

    def adjoint_term(section_no):
        return lax.dynamic_index_in_dim(sorted_terms, section_no, 0, keepdims=False).reshape(
            row_count, width
        )

    def retreat(counter, running):
        moved = shifted_2(running, "blk", -1)
        return moved + adjoint_term(window - 1 - counter)

    adjoint = lax.fori_loop(1, window, retreat, adjoint_term(window - 1))
    for bit_pos in range(rep_size.bit_length() - 1):
        returned = shifted_2(adjoint, "blk", -(window << bit_pos))
        adjoint = jnp.where((replica >> bit_pos) % 2 == 1, returned, adjoint)
    grad_feats = lax.psum_scatter(adjoint, "rep", scatter_dimension=0, tiled=True)
    return (layer_out, grad_feats, grad_weight, grad_bias)


F32, BF16 = jnp.float32, jnp.bfloat16
HALVES = 2
ROW_PARTS = 2


def split(value):
    high = value.astype(BF16)
    return high, (value - high.astype(F32)).astype(BF16)


def dot3(a, b):
    def product(x, y):
        return jnp.dot(x, y, preferred_element_type=F32)

    columns = b[0].shape[1]
    pair = product(a[0], jnp.concatenate([b[0], b[1]], axis=1))
    return pair[:, :columns] + (pair[:, columns:] + product(a[1], b[0]))


def kernel(
    n, m, feats, tiles_hbm, cols_hbm, weight_hbm, bias_hbm, cot_hbm,
    out, gfeats, gweight, gbias,
    tiles, cols, weight, bias, cot,
    xs, s_hi, s_lo, st_hi, st_lo, hpart, hrecv, grad, adj, fold, total, frecv,
    gws, gwr, gwz, gfin, send_sem, recv_sem, load_sem,
):
    p, r = lax.axis_index("blk"), lax.axis_index("rep")
    blocks, slots, size, _ = tiles.shape
    rows = blocks * size
    part, width = cot.shape
    cw = width // HALVES
    piece = width // n
    even = lax.rem(p, 2) == 0
    odd = jnp.logical_not(even)
    moved = r > 0
    always = None

    def both(x, y):
        return jnp.logical_and(x, y)

    def when(cond, action):
        if cond is None:
            action()
        else:
            pl.when(cond)(action)

    nxt = lax.rem(p + 1, n)
    prv = lax.rem(p - 1 + n, n)

    pairs = [
        (tiles_hbm, tiles),
        (cols_hbm, cols),
        (weight_hbm, weight),
        (bias_hbm, bias),
        (cot_hbm, cot),
    ]
    loads = [
        pltpu.make_async_copy(src, dst, load_sem.at[i]) for i, (src, dst) in enumerate(pairs)
    ]
    for made in loads:
        made.start()

    barrier = pltpu.get_barrier_semaphore()
    for d in range(1, n):
        pl.semaphore_signal(barrier, inc=1, device_id={"blk": lax.rem(p + d, n), "rep": r})
    for d in range(1, m):
        pl.semaphore_signal(barrier, inc=1, device_id={"blk": p, "rep": lax.rem(r + d, m)})

    pl.semaphore_wait(barrier, n + m - 2)

    keys, started = {}, []

    def copy(name, src, dst, blk, rep):
        key = keys.setdefault(name, len(keys))
        return pltpu.make_async_remote_copy(
            src_ref=src,
            dst_ref=dst,
            send_sem=send_sem.at[key],
            recv_sem=recv_sem.at[key],
            device_id={"blk": blk, "rep": rep},
        )

    def start(made, cond=always):
        started.append((made, cond))
        when(cond, made.start)

    def flush():
        for made, cond in started:
            when(cond, made.wait_send)
        started.clear()

    def half(c):
        return pl.ds(c * cw, cw)

    ahead = lax.rem(p + 2 * r, n)
    after = lax.rem(p + 2 * r + 1, n)
    to_ahead, to_after = moved, odd

    def to_first(c, src, blk, rep):
        return copy(("a", c), src, xs.at[0, c], blk, rep)

    def to_second(c, src, blk, rep):
        return copy(("b", c), src, xs.at[1, c], blk, rep)

    def send_features(c):
        start(to_second(c, feats.at[:, half(c)], after, r), to_after)
        start(to_first(c, feats.at[:, half(c)], ahead, r), to_ahead)

    send_features(0)
    own = [
        pltpu.make_async_copy(feats.at[:, half(c)], xs.at[0, c], load_sem.at[len(pairs) + c])
        for c in range(HALVES)
    ]

    @pl.when(r == 0)
    def _():
        for c in range(HALVES):
            own[c].start()

    for made in loads:
        made.wait()
    for s in range(2):
        owner = lax.rem(p - 2 * r - s + 2 * n, n)
        for b in range(blocks):
            name = owner * blocks + b
            at = slice((s * blocks + b) * size, (s * blocks + b + 1) * size)
            for i in range(blocks):
                tile = jnp.zeros((size, size), F32)
                for k in range(slots):
                    tile = tile + tiles[i, k] * jnp.where(cols[i, k] == name, 1.0, 0.0)
                high, low = split(tile)
                s_hi[i * size : (i + 1) * size, at] = high
                s_lo[i * size : (i + 1) * size, at] = low
                high, low = split(tile.T)
                st_hi[at, i * size : (i + 1) * size] = high
                st_lo[at, i * size : (i + 1) * size] = low

    flush()
    send_features(1)

    def take_first(c):
        @pl.when(moved)
        def _():
            to_first(c, xs.at[0, c], p, r).wait_recv()

        @pl.when(r == 0)
        def _():
            own[c].wait()

        start(to_second(c, xs.at[0, c], nxt, r), even)

    def product(c, s):
        at = slice(s * rows, (s + 1) * rows)
        return dot3((s_hi[:, at], s_lo[:, at]), split(xs[s, c]))

    hsends = []

    some = part // ROW_PARTS

    def row_part(s):
        return pl.ds(s * some, some)

    def aggregate_sends(c):
        last_half = c == HALVES - 1
        spans = [row_part(s) for s in range(ROW_PARTS)] if last_half else [pl.ds(0, part)]
        for s, span in enumerate(spans):
            made_s = []
            for d in range(m - 1, 0, -1):
                to = lax.rem(r + d, m)
                made = copy(
                    ("c", c, s, d), hpart.at[c, to, span], hrecv.at[c, d - 1, span], p, to
                )
                start(made)
                made_s.append(made)
            hsends.append(made_s)

    for c in range(HALVES):
        take_first(c)
        acc = product(c, 0)
        to_second(c, xs.at[1, c], p, r).wait_recv()
        acc = acc + product(c, 1)
        hpart[c] = acc.reshape(m, part, cw)
        aggregate_sends(c)
    w = split(weight[...])
    wt = split(weight[...].T)

    def aggregate(c, span):
        received = (hrecv[c, 0, span] + hrecv[c, 1, span]) + hrecv[c, 2, span]
        return hpart[c, r, span] + received

    def times_weight(value, c):
        inner = slice(c * cw, (c + 1) * cw)
        return dot3(split(value), (w[0][inner], w[1][inner]))

    for made in hsends[0]:
        made.wait_recv()
    early = aggregate(0, pl.ds(0, part))
    early_pre = times_weight(early, 0) + bias[...]

    forward = list(started)
    started.clear()

    gsends = [[] for _ in range(HALVES)]
    aggs, gpres = [], []
    for s in range(ROW_PARTS):
        here = slice(s * some, (s + 1) * some)
        for made in hsends[1 + s]:
            made.wait_recv()
        late = aggregate(1, row_part(s))
        pre = early_pre[here] + times_weight(late, 1)
        exped = jnp.exp(jnp.minimum(pre, 0.0))
        gpre = cot[here] * jnp.where(pre > 0, 1.0, exped)
        gpre_parts = split(gpre)
        for c in range(HALVES):
            columns = slice(c * cw, (c + 1) * cw)
            grad[c, r, row_part(s)] = dot3(gpre_parts, (wt[0][:, columns], wt[1][:, columns]))
            if c == 0:
                for d in range(m - 1, 0, -1):
                    to = lax.rem(r + d, m)
                    block = grad.at[c, r, row_part(s)]
                    made = copy(("d", c, s, d), block, block, p, to)
                    start(made)
                    gsends[c].append(made)
        out[here] = jnp.where(pre > 0, pre, exped - 1.0)
        aggs.append(jnp.concatenate([early[here], late], axis=1))
        gpres.append(gpre)
    for d in range(m - 1, 0, -1):
        to = lax.rem(r + d, m)
        made = copy(("d", 1, 0, d), grad.at[1, r], grad.at[1, r], p, to)
        start(made)
        gsends[1].append(made)
    agg = jnp.concatenate(aggs, axis=0)
    gpre = jnp.concatenate(gpres, axis=0)
    gpre_parts = split(gpre)

    gw = dot3(split(agg.T), gpre_parts)
    gb = jnp.broadcast_to(jnp.sum(gpre, axis=0, keepdims=True), (8, width))
    for q in range(n):
        gws[q, :piece] = gw[q * piece : (q + 1) * piece]
        gws[q, piece:] = gb
    gwr[p] = gws[p]
    esends = []
    for d in range(1, n):
        to = lax.rem(p + d, n)
        made = copy(("e", d), gws.at[to], gwr.at[p], to, r)
        start(made)
        esends.append(made)

    def weight_sums():
        for made in esends:
            made.wait_recv()
        total_p = gwr[0]
        for q in range(1, n):
            total_p = total_p + gwr[q]
        gwz[r] = total_p
        made_z = []
        for d in range(m - 1, 0, -1):
            to = lax.rem(r + d, m)
            made = copy(("m", d), gwz.at[r], gwz.at[r], p, to)
            start(made)
            made_z.append(made)
        return made_z

    scale = 1.0 / math.sqrt(rows * n)

    def weight_gather(made_z):
        for made in made_z:
            made.wait_recv()
        whole = gwz[0]
        for q in range(1, m):
            whole = whole + gwz[q]
        gfin[p] = whole[:piece] * scale
        gbias[...] = whole[piece : piece + 1] * scale
        made_n = []
        for d in range(1, n):
            to = lax.rem(p + d, n)
            made = copy(("n", d), gfin.at[p], gfin.at[p], to, r)
            start(made)
            made_n.append(made)
        return made_n

    back = lax.rem(p - 2 * r + n, n)
    before = lax.rem(p - 2 * r - 1 + 2 * n, n)
    order = [m - 1 - j for j in range(m)]

    def place(d):
        return lax.rem(r + d, m)

    def to_fold(c, d, blk):
        b = place(d)
        return copy(("f", c, d), adj.at[1, c, b], fold.at[c, b], blk, r)

    def to_total(c, d):
        b = place(d)
        return copy(("k", c, d), adj.at[0, c, b], total.at[c, b], back, r)

    def adjoint(c):
        for made in gsends[c]:
            made.wait_recv()
        g = split(grad[c].reshape(rows, cw))
        adj[1, c] = dot3((st_hi[rows:], st_lo[rows:]), g).reshape(m, part, cw)
        for d in order:
            start(to_fold(c, d, prv), odd)
            start(to_fold(c, d, before), even)
        adj[0, c] = dot3((st_hi[:rows], st_lo[:rows]), g).reshape(m, part, cw)
        for d in order:
            start(to_total(c, d), both(odd, moved))

        @pl.when(even)
        def _():
            for d in order:
                b = place(d)
                to_fold(c, d, prv).wait_recv()
                adj[0, c, b] = adj[0, c, b] + fold[c, b]
                pl.when(moved)(to_total(c, d).start)

        for d in order:
            started.append((to_total(c, d), both(even, moved)))

    def adjoint_reduce(c):
        made_c = []
        for d in order:
            b = place(d)

            @pl.when(moved)
            def _():
                to_total(c, d).wait_recv()

            @pl.when(r == 0)
            def _():
                total[c, b] = adj[0, c, b]

            @pl.when(odd)
            def _():
                to_fold(c, d, prv).wait_recv()
                total[c, b] = total[c, b] + fold[c, b]

            if d:
                made = copy(("l", c, d), total.at[c, b], frecv.at[c, d - 1], p, b)
                start(made)
                made_c.append(made)
        return made_c

    for made, cond in forward:
        when(cond, made.wait_send)
    adjoint(0)
    made_z = weight_sums()
    adjoint(1)
    lsends = [adjoint_reduce(0)]
    made_n = weight_gather(made_z)
    lsends.append(adjoint_reduce(1))
    for c in range(HALVES):
        if c == 1:
            flush()
            for made in made_n:
                made.wait_recv()
            gweight[...] = gfin[...].reshape(width, width)
        for made in lsends[c]:
            made.wait_recv()
        gfeats[:, half(c)] = total[c, r] + ((frecv[c, 0] + frecv[c, 1]) + frecv[c, 2])


def store_results(*refs):
    count = len(refs) // 3
    sources, targets, stages = refs[:count], refs[count : 2 * count], refs[2 * count : 3 * count]
    sems = refs[-1]
    loads = [
        pltpu.make_async_copy(sources[i], stages[i], sems.at[0, i]) for i in range(count)
    ]
    stores = [
        pltpu.make_async_copy(stages[i], targets[i], sems.at[1, i]) for i in range(count)
    ]
    for made in loads:
        made.start()
    for load, store in zip(loads, stores):
        load.wait()
        store.start()
    for made in stores:
        made.wait()


def fast_body(n, m, node_feats, operator_tiles, tile_cols, weight, layer_bias, cotangent):
    blocks, _, size, _ = operator_tiles.shape
    rows = blocks * size
    part, width = cotangent.shape
    cw = width // HALVES
    piece = width // n
    copies = HALVES * (2 + 5 * (m - 1) + 4 * m) + 2 * (n - 1) + (m - 1)
    vmem = pl.BlockSpec(memory_space=pltpu.VMEM)
    shape = jax.ShapeDtypeStruct
    quarter = (HALVES, m, part, cw)
    result = pl.pallas_call(
        functools.partial(kernel, n, m),
        out_shape=(
            shape((part, width), F32),
            shape((part, width), F32),
            shape((width, width), F32),
            shape((1, width), F32),
        ),
        in_specs=[pl.BlockSpec(memory_space=pltpu.HBM)] * 6,
        out_specs=(vmem,) * 4,
        scratch_shapes=[
            pltpu.VMEM(operator_tiles.shape, F32),
            pltpu.SMEM(tile_cols.shape, jnp.int32),
            pltpu.VMEM((width, width), F32),
            pltpu.VMEM((1, width), F32),
            pltpu.VMEM((part, width), F32),
            pltpu.VMEM((2, HALVES, rows, cw), F32),
            pltpu.VMEM((rows, 2 * rows), BF16),
            pltpu.VMEM((rows, 2 * rows), BF16),
            pltpu.VMEM((2 * rows, rows), BF16),
            pltpu.VMEM((2 * rows, rows), BF16),
            pltpu.VMEM(quarter, F32),
            pltpu.VMEM((HALVES, m - 1, part, cw), F32),
            pltpu.VMEM(quarter, F32),
            pltpu.VMEM((2,) + quarter, F32),
            pltpu.VMEM(quarter, F32),
            pltpu.VMEM(quarter, F32),
            pltpu.VMEM((HALVES, m - 1, part, cw), F32),
            pltpu.VMEM((n, piece + 8, width), F32),
            pltpu.VMEM((n, piece + 8, width), F32),
            pltpu.VMEM((m, piece + 8, width), F32),
            pltpu.VMEM((n, piece, width), F32),
            pltpu.SemaphoreType.DMA((copies,)),
            pltpu.SemaphoreType.DMA((copies,)),
            pltpu.SemaphoreType.DMA((5 + HALVES,)),
        ],
        compiler_params=pltpu.CompilerParams(
            collective_id=0, has_side_effects=True, vmem_limit_bytes=63 * 1024 * 1024
        ),
    )(node_feats, operator_tiles, tile_cols, weight, layer_bias.reshape(1, width), cotangent)
    layer_out, grad_feats, grad_weight, grad_bias = pl.pallas_call(
        store_results,
        out_shape=[shape(value.shape, F32) for value in result],
        in_specs=[pl.BlockSpec(memory_space=pl.ANY)] * len(result),
        out_specs=[pl.BlockSpec(memory_space=pl.ANY)] * len(result),
        scratch_shapes=[pltpu.VMEM(value.shape, F32) for value in result]
        + [pltpu.SemaphoreType.DMA((2, len(result)))],
        compiler_params=pltpu.CompilerParams(vmem_limit_bytes=63 * 1024 * 1024),
    )(*result)
    return layer_out, grad_feats, grad_weight, grad_bias.reshape(width)


def solution(mesh):
    n, m = mesh.shape["blk"], mesh.shape["rep"]
    fits = n == 2 * m and m == 4
    return jax.shard_map(
        functools.partial(fast_body, n, m) if fits else body,
        mesh=mesh,
        in_specs=(
            P("blk", None),
            P("blk", "rep", None, None),
            P("blk", "rep"),
            P(),
            P(),
            P(("blk", "rep"), None),
        ),
        out_specs=(P(("blk", "rep"), None), P(("blk", "rep"), None), P(), P()),
        check_vma=False,
    )
```
